512 devices in a mesh: pair: 32 (over x, z_lo), pix: 16 (over y, z_hi, core).
Axes of the slice: x: 4, y: 4, z: 16 (z_hi: 2, z_lo: 8; z = z_hi * 8 + z_lo), core: 2. Of those that a mesh axis runs over, the one named last changes fastest.
Arguments:
- frame_one: bfloat16 [32, 6144, 128], P('pair', 'pix'), may hold values from -6 to 6
- frame_two: bfloat16 [32, 6144, 128], P('pair', 'pix'), may hold values from -6 to 6
- weight: bfloat16 [128, 128], replicated, may hold values from -0.5 to 0.5
- flow_grad: float32 [32, 2, 6144], P('pair', None, 'pix'), may hold values from -6 to 6
Outputs:
- flow: float32 [32, 2, 6144], P('pair', None, 'pix')
- grad_frame_one: bfloat16 [32, 6144, 128], P('pair', 'pix')
- grad_frame_two: bfloat16 [32, 6144, 128], P('pair', 'pix')
- weight_grad: float32 [128, 128], P('pair')
The draws below stay inside these ranges and needn't reach their ends.
All inputs are finite; a program needn't handle non-finite values.
Results may differ from the reference program's by a relative error of at most 0.024.
Values may be sent and summed in bfloat16 or wider, within the bound.
No kernel may reach another device: no remote copies, remote signals or barrier semaphores. Data moves between devices by JAX's collectives and lax.ppermute only.
A program may use at most 64 MiB of HBM per device.

```python
import jax
import jax.numpy as jnp
from jax import lax

C = 128
PIX_DEV = 384
COLS = 128
FRAME_PIX = 6144
PAIRS = 32
N_PIX = 16


def draw_frame_one(key, part):
    key = jax.random.fold_in(key, 1)
    values = jnp.clip(jax.random.normal(key, (PAIRS, PIX_DEV * N_PIX, C), jnp.float32), -6.0, 6.0)
    return values.astype(jnp.bfloat16)


def draw_frame_two(key, part):
    key = jax.random.fold_in(key, 3)
    values = jnp.clip(jax.random.normal(key, (PAIRS, PIX_DEV * N_PIX, C), jnp.float32), -6.0, 6.0)
    return values.astype(jnp.bfloat16)


def shard_levels(stream_key, dims, cuts, low, top_value):
    def one(position, parts):
        steps = jax.random.uniform(jax.random.fold_in(jax.random.fold_in(stream_key, 6), position), (parts,), jnp.float32, low / len(cuts), top_value / len(cuts))
        return jnp.repeat(jnp.exp(steps), dims[position] // parts).reshape((-1,) + (1,) * (len(dims) - position - 1))

    gain = one(*cuts[0])
    for cut in cuts[1:]:
        gain = gain * one(*cut)
    return gain


def scatter_about(own_key, extent, scale, bound, shards=(), kind=jnp.bfloat16):
    result = jax.random.normal(own_key, extent, jnp.float32) * scale
    if len(shards) > 0:
        result = shard_levels(own_key, extent, shards, -0.22, 0.18) * result
    return jnp.clip(result, min=-bound, max=bound).astype(kind)


def setup_inputs(seed: int = 0) -> dict:
    splits = jax.random.split(jax.random.key(seed), 5)
    frame_one = draw_frame_one(jax.random.fold_in(splits[4], 71), 0)
    frame_two = draw_frame_two(jax.random.fold_in(splits[4], 71), 0)
    weight = scatter_about(splits[2], (C, C), C ** -0.5, 0.5)
    flow_grad = scatter_about(splits[3], (PAIRS, 2, FRAME_PIX), 1.0, 6.0, ((0, 32), (2, 16)), jnp.float32)
    return dict(frame_one=frame_one, frame_two=frame_two, weight=weight, flow_grad=flow_grad)


def coordinates(index):
    frame_rows = PIX_DEV * N_PIX // COLS
    column = (index % COLS).astype(jnp.float32)
    row = (index // COLS).astype(jnp.float32)
    return 2.0 * column / (COLS - 1) - 1.0, 2.0 * row / (frame_rows - 1) - 1.0


def match_pair(first, second, cotangent, weight):
    npixels = PIX_DEV * N_PIX
    scale = C ** -0.5
    feat_one = jnp.dot(first, weight, preferred_element_type=jnp.float32).astype(jnp.bfloat16)
    feat_two = jnp.dot(second, weight, preferred_element_type=jnp.float32).astype(jnp.bfloat16)
    key_x, key_y = coordinates(jnp.arange(npixels, dtype=jnp.int32))
    blocks_one = feat_one.reshape(N_PIX, PIX_DEV, C)
    blocks_grad = cotangent.reshape(2, N_PIX, PIX_DEV).transpose(1, 0, 2)
    starts = jnp.arange(N_PIX, dtype=jnp.int32) * PIX_DEV

    def visit(carried, inputs):
        query, grads, start = inputs
        query_x, query_y = coordinates(start + jnp.arange(PIX_DEV, dtype=jnp.int32))
        score = jnp.dot(query, feat_two.T, preferred_element_type=jnp.float32) * scale
        peak = jnp.max(score, axis=1, keepdims=True)
        weights = jnp.exp(score - peak)
        total = jnp.sum(weights, axis=1)
        mean_x = jnp.sum(weights * key_x[None, :], axis=1) / total
        mean_y = jnp.sum(weights * key_y[None, :], axis=1) / total
        prob = weights / total[:, None]
        flow_block = jnp.stack([mean_x - query_x, mean_y - query_y])
        center = grads[0] * mean_x + grads[1] * mean_y
        slope = ((grads[0][:, None] * key_x[None, :] + grads[1][:, None] * key_y[None, :] - center[:, None]) * prob * scale).astype(jnp.bfloat16)
        grad_query = jnp.dot(slope, feat_two, preferred_element_type=jnp.float32)
        carried = carried + jnp.dot(slope.T, query, preferred_element_type=jnp.float32)
        return carried, (flow_block, grad_query)

    grad_two, (flows, grad_ones) = lax.scan(visit, jnp.zeros((npixels, C), jnp.float32), (blocks_one, blocks_grad, starts))
    flow = flows.transpose(1, 0, 2).reshape(2, npixels)
    grad_one = grad_ones.reshape(npixels, C).astype(jnp.bfloat16)
    grad_two = grad_two.astype(jnp.bfloat16)
    back_one = jnp.dot(grad_one, weight.T, preferred_element_type=jnp.float32).astype(jnp.bfloat16)
    back_two = jnp.dot(grad_two, weight.T, preferred_element_type=jnp.float32).astype(jnp.bfloat16)
    partial_grad = jnp.dot(first.T, grad_one, preferred_element_type=jnp.float32) + jnp.dot(second.T, grad_two, preferred_element_type=jnp.float32)
    return flow, back_one, back_two, partial_grad


def reference(frame_one, frame_two, weight, flow_grad):
    def per_pair(total, inputs):
        flow, back_one, back_two, partial_grad = match_pair(inputs[0], inputs[1], inputs[2], weight)
        return total + partial_grad, (flow, back_one, back_two)

    weight_grad, (flow, grad_frame_one, grad_frame_two) = lax.scan(per_pair, jnp.zeros((C, C), jnp.float32), (frame_one, frame_two, flow_grad))
    return flow, grad_frame_one, grad_frame_two, weight_grad
```

```python
import functools

import jax
import jax.numpy as jnp
from jax import lax
from jax.experimental import pallas as pl
from jax.experimental.pallas import tpu as pltpu
from jax.sharding import PartitionSpec as P

COLS = 128
LANES = 128
SUB = 32
LOG2E = 1.4426950408889634


def dot(a, b, contract):
    return lax.dot_general(a, b, (contract, ((), ())), preferred_element_type=jnp.float32)


def turned(a):
    return a.astype(jnp.float32).T.astype(jnp.bfloat16)


def lane_iota(rows):
    return lax.broadcasted_iota(jnp.int32, (rows, LANES), 1)


def match_kernel(
    frame_rows, scale,
    own_keys, far_keys, q_own, q_far, g_own, g_far, weight,
    flow, back_one, payload,
    keys, score, prob, feat_q, grads, stat, both_grads, low, turned_q, turned_g,
):
    groups, blocks, count, chans = 2, own_keys.shape[0], q_own.shape[0], q_own.shape[1]
    half = blocks * count
    rows_per_block = count // COLS
    unit = scale * LOG2E
    here = lax.axis_index("pix")
    z_hi = (here // 2) % 2
    w = weight[...]

    def frame_row(group, block, row):
        z = z_hi if group == 0 else 1 - z_hi
        index = (block // 2) * 4 + block % 2 + 2 * z
        return (index * rows_per_block + row).astype(jnp.float32)

    for group, source in ((0, own_keys), (1, far_keys)):
        def project(block, _, group=group, source=source):
            raw = source[block]
            start = pl.multiple_of(group * half + block * count, count)
            keys[pl.ds(start, count), 0:chans] = dot(raw, w, ((1,), (0,))).astype(jnp.bfloat16)
            keys[pl.ds(start, count), chans : 2 * chans] = raw
            return 0

        lax.fori_loop(0, blocks, project, 0)
    feat_q[0:count, :] = dot(q_own[...], w, ((1,), (0,))).astype(jnp.bfloat16)
    feat_q[count : 2 * count, :] = dot(q_far[...], w, ((1,), (0,))).astype(jnp.bfloat16)

    for part, source in ((0, g_own), (1, g_far)):
        padded = jnp.concatenate([source[...], jnp.zeros((LANES - 2, count), jnp.float32)], axis=0)
        grads[part * count : (part + 1) * count, :] = padded.T

    lane = lane_iota(SUB)
    lane_f = lane.astype(jnp.float32)
    tiles = half // LANES

    for part in range(2):
        for group in range(groups):
            def scores(block, _, part=part, group=group):
                start = pl.multiple_of(group * half + block * count, count)
                score[:, pl.ds(pl.multiple_of(block * count, LANES), count)] = dot(
                    feat_q[part * count : (part + 1) * count, :],
                    keys[pl.ds(start, count), 0:chans],
                    ((1,), (1,)),
                )
                return 0

            lax.fori_loop(0, blocks, scores, 0)

            def weigh(step, _, part=part, group=group):
                rows = pl.ds(pl.multiple_of(step * SUB, SUB), SUB)
                top = score[rows, 0:LANES]
                for j in range(1, tiles):
                    top = jnp.maximum(top, score[rows, j * LANES : (j + 1) * LANES])
                peak = jnp.max(top, axis=1, keepdims=True) * unit
                total = jnp.zeros((SUB, LANES), jnp.float32)
                total_row = jnp.zeros((SUB, LANES), jnp.float32)
                for j in range(tiles):
                    at = slice(j * LANES, (j + 1) * LANES)
                    p = jnp.exp2(score[rows, at] * unit - peak)
                    total = total + p
                    total_row = total_row + p * frame_row(group, j // rows_per_block, j % rows_per_block)
                    if part == 0:
                        prob[rows, group * half + j * LANES : group * half + (j + 1) * LANES] = p.astype(jnp.bfloat16)
                in_all = jnp.sum(total, axis=1, keepdims=True)
                in_x = jnp.sum(total * lane_f, axis=1, keepdims=True)
                in_y = jnp.sum(total_row, axis=1, keepdims=True)
                packed = jnp.where(lane == 0, peak, jnp.where(lane == 1, in_all, jnp.where(lane == 2, in_x, in_y)))
                stat[group, pl.ds(pl.multiple_of(part * count + step * SUB, SUB), SUB), :] = packed
                return 0

            lax.fori_loop(0, count // SUB, weigh, 0)

        def finish(step, _, part=part):
            rows = pl.ds(pl.multiple_of(step * SUB, SUB), SUB)
            q_rows = pl.ds(pl.multiple_of(part * count + step * SUB, SUB), SUB)
            near, far = stat[0, q_rows, :], stat[1, q_rows, :]
            peak_near, peak_far = near[:, 0:1], far[:, 0:1]
            peak = jnp.maximum(peak_near, peak_far)
            by_near, by_far = jnp.exp2(peak_near - peak), jnp.exp2(peak_far - peak)
            in_all = by_near * near[:, 1:2] + by_far * far[:, 1:2]
            mean_col = (by_near * near[:, 2:3] + by_far * far[:, 2:3]) / in_all
            mean_row = (by_near * near[:, 3:4] + by_far * far[:, 3:4]) / in_all
            mean_x = 2.0 * mean_col / (COLS - 1) - 1.0
            mean_y = 2.0 * mean_row / (frame_rows - 1) - 1.0
            grad = grads[q_rows, :]
            grad_x, grad_y = grad[:, 0:1] * scale, grad[:, 1:2] * scale
            center = grad_x * mean_x + grad_y * mean_y
            level = peak + jnp.log2(in_all)
            packed = jnp.where(lane == 0, level, jnp.where(lane == 1, grad_x, jnp.where(lane == 2, grad_y,
                jnp.where(lane == 3, center, jnp.where(lane == 4, mean_x, mean_y)))))
            grads[q_rows, :] = packed
            if part == 0:
                key_x = 2.0 * lane_f / (COLS - 1) - 1.0
                for group, factor in ((0, by_near / in_all), (1, by_far / in_all)):
                    base = (grad_x * key_x - center) * factor
                    tilt = jnp.broadcast_to(grad_y * factor, (SUB, LANES))
                    for j in range(tiles):
                        at = slice(group * half + j * LANES, group * half + (j + 1) * LANES)
                        key_y = 2.0 * frame_row(group, j // rows_per_block, j % rows_per_block) / (frame_rows - 1) - 1.0
                        slope = prob[rows, at].astype(jnp.float32) * (base + tilt * key_y)
                        prob[rows, at] = slope.astype(jnp.bfloat16)
            return 0

        lax.fori_loop(0, count // SUB, finish, 0)

        if part == 0:
            both_grads[...] = jnp.zeros_like(both_grads)

            def gather_grads(block, _):
                start = pl.multiple_of(block * count, count)
                both_grads[...] += dot(
                    prob[:, pl.ds(pl.multiple_of(block * count, LANES), count)],
                    keys[pl.ds(start, count), :],
                    ((1,), (0,)),
                )
                return 0

            lax.fori_loop(0, groups * blocks, gather_grads, 0)
            low[...] = both_grads[...].astype(jnp.bfloat16)
            turned_q[...] = turned(q_own[...])
            turned_g[...] = turned(low[:, chans : 2 * chans])

    back_one[...] = dot(low[:, 0:chans], w, ((1,), (1,))).astype(jnp.bfloat16)
    term = dot(turned_q[...], low[:, 0:chans], ((1,), (0,)))
    term = term + dot(turned_g[...], feat_q[0:count, :], ((1,), (0,)))
    flipped = grads[...].T
    q_lane = lax.broadcasted_iota(jnp.int32, (1, count), 1)
    q_x = 2.0 * (q_lane % COLS).astype(jnp.float32) / (COLS - 1) - 1.0
    q_y = 2.0 * (q_lane // COLS + here * rows_per_block).astype(jnp.float32) / (frame_rows - 1) - 1.0
    flow[0:1, :] = flipped[4:5, 0:count] - q_x
    flow[1:2, :] = flipped[5:6, 0:count] - q_y

    width = 2 * count // LANES
    payload[0, 0:chans, :] = term
    for which in range(4):
        for j in range(width):
            payload[0, chans + which * width + j : chans + which * width + j + 1, :] = flipped[
                which : which + 1, j * LANES : (j + 1) * LANES
            ]

    def copies(device, _):
        payload[device] = payload[0]
        return 0

    lax.fori_loop(1, blocks, copies, 0)


def keys_kernel(
    frame_rows, scale,
    near_q, far_q, near_stat, frame_two, weight,
    back_two,
    column, slope, acc, feat_q,
):
    blocks, count, chans = near_q.shape
    unit = scale * LOG2E
    here = lax.axis_index("pix")
    rows_per_block = count // COLS
    width = 2 * count // LANES
    w = weight[...]
    feat_k = dot(frame_two[...], w, ((1,), (0,))).astype(jnp.bfloat16)
    sub = lax.broadcasted_iota(jnp.int32, (count, LANES), 0)
    column[...] = 2.0 * (sub % COLS).astype(jnp.float32) / (COLS - 1) - 1.0
    tiles = count // LANES
    acc[...] = jnp.zeros_like(acc)

    def visit(block, _):
        for part, source in ((0, near_q), (1, far_q)):
            feat = dot(source[block, 0:count, :], w, ((1,), (0,))).astype(jnp.bfloat16)
            feat_q[...] = feat
            score = dot(feat_k, feat_q[...], ((1,), (1,)))
            for j in range(tiles):
                at = part * tiles + j
                level = near_stat[block, at : at + 1, :]
                grad_x = near_stat[block, width + at : width + at + 1, :]
                grad_y = near_stat[block, 2 * width + at : 2 * width + at + 1, :]
                center = near_stat[block, 3 * width + at : 3 * width + at + 1, :]
                for row in range(rows_per_block):
                    key_y = 2.0 * (here * rows_per_block + row).astype(jnp.float32) / (frame_rows - 1) - 1.0
                    offset = grad_y * key_y - center
                    for step in range(COLS // SUB):
                        rows = slice(row * COLS + step * SUB, row * COLS + (step + 1) * SUB)
                        p = jnp.exp2(score[rows, j * LANES : (j + 1) * LANES] * unit - level)
                        value = p * (column[rows, :] * grad_x + offset)
                        slope[rows, j * LANES : (j + 1) * LANES] = value.astype(jnp.bfloat16)
            acc[...] += dot(slope[...], feat_q[...], ((1,), (0,)))
        return 0

    lax.fori_loop(0, blocks, visit, 0)
    back_two[...] = dot(acc[...].astype(jnp.bfloat16), w, ((1,), (1,))).astype(jnp.bfloat16)


def whole(*shape):
    return pl.BlockSpec(shape, lambda i: (0,) * len(shape))


def on_device(frame_one, frame_two, weight, flow_grad):
    _, count, chans = frame_one.shape
    devices = lax.axis_size("pix")
    blocks = devices // 2
    frame_rows = count * devices // COLS
    scale = chans ** (-0.5)
    near = [[i for i in range(devices) if (i // 2) % 2 == z] for z in range(2)]
    across = [(i, i ^ 2) for i in range(devices)]

    one, two, grad = frame_one[0], frame_two[0], flow_grad[0]
    with jax.named_scope("frame_two_across"):
        far_two = lax.ppermute(two, "pix", across)
    with jax.named_scope("frame_one_across"):
        far_one = lax.ppermute(one, "pix", across)
        far_grad = lax.ppermute(grad, "pix", across)
    with jax.named_scope("near_gather"):
        near_both = lax.all_gather(jnp.concatenate([one, two], axis=0), "pix", axis=0, axis_index_groups=near)
    with jax.named_scope("far_two_gather"):
        far_keys = lax.all_gather(far_two, "pix", axis=0, axis_index_groups=near)
    with jax.named_scope("far_one_gather"):
        padded = jnp.concatenate([far_one, far_one[0:LANES]], axis=0)
        far_queries = lax.all_gather(padded, "pix", axis=0, axis_index_groups=near)

    width = 2 * count // LANES
    load = chans + 4 * width
    params = pltpu.CompilerParams(vmem_limit_bytes=40 * 1024 * 1024)
    half = blocks * count
    flow, back_one, payload = pl.pallas_call(
        functools.partial(match_kernel, frame_rows, scale),
        grid=(1,),
        in_specs=[
            pl.BlockSpec((blocks, count, chans), lambda i: (0, 1, 0)),
            whole(blocks, count, chans),
            whole(count, chans),
            whole(count, chans),
            whole(2, count),
            whole(2, count),
            whole(chans, chans),
        ],
        out_specs=[whole(2, count), whole(count, chans), whole(blocks, load, LANES)],
        out_shape=[
            jax.ShapeDtypeStruct((2, count), jnp.float32),
            jax.ShapeDtypeStruct((count, chans), jnp.bfloat16),
            jax.ShapeDtypeStruct((blocks, load, LANES), jnp.float32),
        ],
        scratch_shapes=[
            pltpu.VMEM((2 * half, 2 * chans), jnp.bfloat16),
            pltpu.VMEM((count, half), jnp.float32),
            pltpu.VMEM((count, 2 * half), jnp.bfloat16),
            pltpu.VMEM((2 * count, chans), jnp.bfloat16),
            pltpu.VMEM((2 * count, LANES), jnp.float32),
            pltpu.VMEM((2, 2 * count, LANES), jnp.float32),
            pltpu.VMEM((count, 2 * chans), jnp.float32),
            pltpu.VMEM((count, 2 * chans), jnp.bfloat16),
            pltpu.VMEM((chans, count), jnp.bfloat16),
            pltpu.VMEM((chans, count), jnp.bfloat16),
        ],
        compiler_params=params,
        cost_estimate=pl.CostEstimate(flops=6 * 2 * count * 2 * half * chans, bytes_accessed=8 * 2**20, transcendentals=0),
        name="match",
    )(near_both, far_keys, one, far_one, grad, far_grad, weight)

    with jax.named_scope("statistics_exchange"):
        arrived = lax.all_to_all(payload, "pix", 0, 0, axis_index_groups=near)
    with jax.named_scope("weight_terms"):
        term = jnp.sum(arrived[:, 0:chans, :], axis=0)
        pairs = lax.axis_size("pair")
        chunk = chans // pairs
        sent = jnp.repeat(term.reshape(pairs, chunk, chans), 2, axis=0)
        planes = [
            [p * devices + z * 2 + r for p in range(pairs) for z in range(2)]
            for r in [y * 4 + c for y in range(devices // 4) for c in range(2)]
        ]
        terms = lax.all_to_all(sent, ("pair", "pix"), 0, 0, axis_index_groups=planes)
        weight_grad = jnp.sum(terms, axis=0)

    back_two = pl.pallas_call(
        functools.partial(keys_kernel, frame_rows, scale),
        grid=(1,),
        in_specs=[
            pl.BlockSpec((blocks, count, chans), lambda i: (0, 0, 0)),
            whole(blocks, count + LANES, chans),
            whole(blocks, 4 * width, LANES),
            whole(count, chans),
            whole(chans, chans),
        ],
        out_specs=whole(count, chans),
        out_shape=jax.ShapeDtypeStruct((count, chans), jnp.bfloat16),
        scratch_shapes=[
            pltpu.VMEM((count, LANES), jnp.float32),
            pltpu.VMEM((count, count), jnp.bfloat16),
            pltpu.VMEM((count, chans), jnp.float32),
            pltpu.VMEM((count, chans), jnp.bfloat16),
        ],
        compiler_params=params,
        cost_estimate=pl.CostEstimate(flops=6 * count * 2 * half * chans, bytes_accessed=8 * 2**20, transcendentals=0),
        name="keys",
    )(near_both, far_queries, arrived[:, chans:, :], two, weight)
    return (flow[None], back_one[None], back_two[None], weight_grad)


def solution(mesh):
    return jax.shard_map(
        on_device,
        mesh=mesh,
        in_specs=(P("pair", "pix", None), P("pair", "pix", None), P(), P("pair", None, "pix")),
        out_specs=(
            P("pair", None, "pix"),
            P("pair", "pix", None),
            P("pair", "pix", None),
            P("pair", None),
        ),
        check_vma=False,
    )
```

```python
import functools

import jax
import jax.numpy as jnp
from jax import lax
from jax.experimental import pallas as pl
from jax.experimental.pallas import tpu as pltpu
from jax.sharding import PartitionSpec as P

COLS = 128
LANES = 128
SUB = 32
GRAD_ROWS = 16
STAT_ROWS = 32
LOG2E = 1.4426950408889634


def dot(a, b, contract):
    return lax.dot_general(a, b, (contract, ((), ())), preferred_element_type=jnp.float32)


def many(low, high, each, step):
    def body(i, _):
        for k in range(each):
            step(low + i * each + k, 0)
        return 0

    lax.fori_loop(0, (high - low) // each, body, 0)


def turned(a):
    return a.astype(jnp.float32).T.astype(jnp.bfloat16)


def lane_iota(rows):
    return lax.broadcasted_iota(jnp.int32, (rows, LANES), 1)


def parted(value):
    high = value.astype(jnp.bfloat16)
    rest = value - high.astype(jnp.float32)
    middle = rest.astype(jnp.bfloat16)
    return high, middle, (rest - middle.astype(jnp.float32)).astype(jnp.bfloat16)


def joined(ref, start, rows):
    total = ref[start : start + rows, :].astype(jnp.float32)
    for part in (1, 2):
        total = total + ref[start + part * rows : start + (part + 1) * rows, :].astype(jnp.float32)
    return total


def pack_kernel(one, two, grad, out, spread):
    count = one.shape[0]
    wide = count // LANES
    out[0:count, :] = one[...]
    out[count : 2 * count, :] = two[...]
    spread[...] = jnp.zeros_like(spread)
    for which in range(2):
        for j in range(wide):
            spread[which * wide + j : which * wide + j + 1, :] = grad[which : which + 1, j * LANES : (j + 1) * LANES]
    for part, value in enumerate(parted(spread[...])):
        start = 2 * count + part * GRAD_ROWS
        out[start : start + GRAD_ROWS, :] = value


def match_kernel(
    frame_rows, scale,
    near_keys, far_keys, q_own, g_own, packed_far, weight,
    flow, back_one, payload,
    keys, score_far, score_own, prob, feat_q, grads, top, total, total_row, base, tilt, both, low, turned_q, turned_g, wide_grad, spread,
):
    blocks, count, chans = near_keys.shape[0], q_own.shape[0], q_own.shape[1]
    visits = 2 * blocks
    rows_per_block = count // COLS
    tiles = visits * rows_per_block
    unit = scale * LOG2E
    here = lax.axis_index("pix")
    z_hi = (here // 2) % 2
    w = weight[...]

    def frame_row(block, row):
        z = z_hi if block < blocks else 1 - z_hi
        place = block % blocks
        index = (place // 2) * 4 + place % 2 + 2 * z
        return (index * rows_per_block + row).astype(jnp.float32)

    feat_q[0:count, :] = dot(q_own[...], w, ((1,), (0,))).astype(jnp.bfloat16)
    feat_q[count : 2 * count, :] = dot(packed_far[0:count, :], w, ((1,), (0,))).astype(jnp.bfloat16)
    wide_grad[...] = jnp.zeros_like(wide_grad)
    wide_grad[0:2, 0:count] = g_own[...]
    far_grad = joined(packed_far, 2 * count, GRAD_ROWS)
    for which in range(2):
        for j in range(rows_per_block):
            wide_grad[which : which + 1, count + j * LANES : count + (j + 1) * LANES] = far_grad[
                which * rows_per_block + j : which * rows_per_block + j + 1, :
            ]
    grads[...] = wide_grad[...].T

    def scores(block, queries, part, score):
        start = pl.multiple_of(block * count, count)
        out = dot(queries, keys[pl.ds(start, count), 0:chans], ((1,), (1,)))
        score[:, pl.ds(start, count)] = out
        rows = slice(part * count, (part + 1) * count)
        best = top[rows, :]
        for j in range(rows_per_block):
            best = jnp.maximum(best, out[:, j * LANES : (j + 1) * LANES])
        top[rows, :] = best

    def weigh(start, size, part, score, keep):
        rows = pl.ds(start, size)
        q_rows = pl.ds(part * count + start, size)
        peak = top[q_rows, :]
        in_all = jnp.zeros((size, LANES), jnp.float32)
        in_row = jnp.zeros((size, LANES), jnp.float32)
        for j in range(tiles):
            p = jnp.exp2(score[rows, j * LANES : (j + 1) * LANES] * unit - peak)
            in_all = in_all + p
            in_row = in_row + p * frame_row(j // rows_per_block, j % rows_per_block)
            if keep:
                prob[rows, j * LANES : (j + 1) * LANES] = p.astype(jnp.bfloat16)
        total[q_rows, :] = in_all
        total_row[q_rows, :] = in_row

    def settle(part):
        rows = slice(part * count, (part + 1) * count)
        top[rows, :] = jnp.broadcast_to(jnp.max(top[rows, :], axis=1, keepdims=True) * unit, (count, LANES))

    top[...] = jnp.full_like(top, -jnp.inf)

    def first(block, _):
        start = pl.multiple_of(block * count, count)
        place = lax.rem(block, blocks)
        raw = jnp.where(block < blocks, near_keys[place], far_keys[place])
        keys[pl.ds(start, count), 0:chans] = dot(raw, w, ((1,), (0,))).astype(jnp.bfloat16)
        keys[pl.ds(start, count), chans : 2 * chans] = raw
        scores(block, feat_q[count : 2 * count, :], 1, score_far)
        return 0

    many(0, visits, 8, first)
    settle(1)

    def second(block, _):
        scores(block, feat_q[0:count, :], 0, score_own)
        size = count // visits
        weigh(pl.multiple_of(block * size, size), size, 1, score_far, False)
        return 0

    many(0, visits, 8, second)
    settle(0)

    def third(step, _):
        weigh(pl.multiple_of(step * SUB, SUB), SUB, 0, score_own, True)
        return 0

    many(0, count // SUB, 6, third)

    lane = lane_iota(2 * count)
    lane_f = lane.astype(jnp.float32)
    peak = top[:, 0:1]
    in_all = jnp.sum(total[...], axis=1, keepdims=True)
    mean_x = 2.0 * (jnp.sum(total[...] * lane_f, axis=1, keepdims=True) / in_all) / (COLS - 1) - 1.0
    mean_y = 2.0 * (jnp.sum(total_row[...], axis=1, keepdims=True) / in_all) / (frame_rows - 1) - 1.0
    grad = grads[...]
    grad_x, grad_y = grad[:, 0:1] * scale, grad[:, 1:2] * scale
    center = grad_x * mean_x + grad_y * mean_y
    level = peak + jnp.log2(in_all)
    grads[...] = jnp.where(lane == 0, level, jnp.where(lane == 1, grad_x, jnp.where(lane == 2, grad_y,
        jnp.where(lane == 3, center, jnp.where(lane == 4, mean_x, mean_y)))))
    key_x = 2.0 * lane_f[0:count, :] / (COLS - 1) - 1.0
    share = 1.0 / in_all[0:count, :]
    base[...] = (grad_x[0:count, :] * key_x - center[0:count, :]) * share
    tilt[...] = jnp.broadcast_to(grad_y[0:count, :] * share, (count, LANES))
    both[...] = jnp.zeros_like(both)

    def slopes(block):
        start = pl.multiple_of(block * count, count)
        z = jnp.where(block < blocks, z_hi, 1 - z_hi)
        place = lax.rem(block, blocks)
        index = lax.div(place, 2) * 4 + lax.rem(place, 2) + 2 * z
        for j in range(rows_per_block):
            at = pl.ds(pl.multiple_of(start + j * LANES, LANES), LANES)
            key_y = 2.0 * (index * rows_per_block + j).astype(jnp.float32) / (frame_rows - 1) - 1.0
            for step in range(count // SUB):
                rows = slice(step * SUB, (step + 1) * SUB)
                value = prob[rows, at].astype(jnp.float32) * (base[rows, :] + tilt[rows, :] * key_y)
                prob[rows, at] = value.astype(jnp.bfloat16)

    def collect(block):
        start = pl.multiple_of(block * count, count)
        both[...] += dot(prob[:, pl.ds(start, count)], keys[pl.ds(start, count), :], ((1,), (0,)))

    slopes(0)

    def fourth(block, _):
        collect(block)
        slopes(block + 1)
        return 0

    many(0, visits - 1, 15, fourth)
    collect(visits - 1)
    low[...] = both[...].astype(jnp.bfloat16)
    turned_q[...] = turned(q_own[...])
    turned_g[...] = turned(low[:, chans : 2 * chans])
    back_one[...] = dot(low[:, 0:chans], w, ((1,), (1,))).astype(jnp.bfloat16)
    term = dot(turned_q[...], low[:, 0:chans], ((1,), (0,)))
    term = term + dot(turned_g[...], feat_q[0:count, :], ((1,), (0,)))

    flipped = grads[...].T
    q_lane = lax.broadcasted_iota(jnp.int32, (1, count), 1)
    q_x = 2.0 * (q_lane % COLS).astype(jnp.float32) / (COLS - 1) - 1.0
    q_y = 2.0 * (q_lane // COLS + here * rows_per_block).astype(jnp.float32) / (frame_rows - 1) - 1.0
    flow[0:1, :] = flipped[4:5, 0:count] - q_x
    flow[1:2, :] = flipped[5:6, 0:count] - q_y

    width = 2 * count // LANES
    payload[0, 0:chans, :] = term.astype(jnp.bfloat16)
    spread[...] = jnp.zeros_like(spread)
    for which in range(4):
        for j in range(width):
            spread[which * width + j : which * width + j + 1, :] = flipped[which : which + 1, j * LANES : (j + 1) * LANES]
    for part, value in enumerate(parted(spread[...])):
        payload[0, chans + part * STAT_ROWS : chans + (part + 1) * STAT_ROWS, :] = value

    def copies(device, _):
        payload[device] = payload[0]
        return 0

    lax.fori_loop(1, blocks, copies, 0)


def keys_kernel(
    frame_rows, scale,
    near_q, far_q, arrived, frame_two, weight,
    back_two,
    column, feat_q, feat_k, score_a, score_b, slope_a, slope_b, acc, stat,
):
    blocks, count, chans = near_q.shape
    unit = scale * LOG2E
    here = lax.axis_index("pix")
    rows_per_block = count // COLS
    width = 2 * count // LANES
    w = weight[...]
    feat_k[...] = dot(frame_two[...], w, ((1,), (0,))).astype(jnp.bfloat16)
    sub = lax.broadcasted_iota(jnp.int32, (COLS, LANES), 0)
    column[...] = 2.0 * sub.astype(jnp.float32) / (COLS - 1) - 1.0
    tiles = count // LANES
    acc[...] = jnp.zeros_like(acc)
    for block in range(blocks):
        stat[block] = joined(arrived.at[block], chans, STAT_ROWS)

    def project(block, _):
        for part, source in ((0, near_q), (1, far_q)):
            start = pl.multiple_of((block * 2 + part) * count, count)
            feat_q[pl.ds(start, count), :] = dot(source[block, 0:count, :], w, ((1,), (0,))).astype(jnp.bfloat16)
        return 0

    many(0, blocks, 4, project)

    def queries(visit):
        return feat_q[pl.ds(pl.multiple_of(visit * count, count), count), :]

    def scores(visit, score):
        score[...] = dot(feat_k[...], queries(visit), ((1,), (1,)))

    def slopes(block, part, score, slope):
        for j in range(tiles):
            at = part * tiles + j
            level = stat[block, at : at + 1, :]
            grad_x = stat[block, width + at : width + at + 1, :]
            grad_y = stat[block, 2 * width + at : 2 * width + at + 1, :]
            center = stat[block, 3 * width + at : 3 * width + at + 1, :]
            for row in range(rows_per_block):
                key_y = 2.0 * (here * rows_per_block + row).astype(jnp.float32) / (frame_rows - 1) - 1.0
                offset = grad_y * key_y - center
                for step in range(COLS // SUB):
                    rows = slice(row * COLS + step * SUB, row * COLS + (step + 1) * SUB)
                    p = jnp.exp2(score[rows, j * LANES : (j + 1) * LANES] * unit - level)
                    value = p * (column[step * SUB : (step + 1) * SUB, :] * grad_x + offset)
                    slope[rows, j * LANES : (j + 1) * LANES] = value.astype(jnp.bfloat16)

    def collect(visit, slope):
        acc[...] += dot(slope[...], queries(visit), ((1,), (0,)))

    scores(0, score_a)
    slope_b[...] = jnp.zeros_like(slope_b)

    def visit(block, _):
        first, second = 2 * block, 2 * block + 1
        scores(second, score_b)
        slopes(block, 0, score_a, slope_a)
        collect(jnp.maximum(second - 2, 0), slope_b)
        scores(jnp.minimum(first + 2, 2 * blocks - 1), score_a)
        slopes(block, 1, score_b, slope_b)
        collect(first, slope_a)
        return 0

    many(0, blocks, 4, visit)
    collect(2 * blocks - 1, slope_b)
    back_two[...] = dot(acc[...].astype(jnp.bfloat16), w, ((1,), (1,))).astype(jnp.bfloat16)


def whole(*shape):
    return pl.BlockSpec(shape, lambda i: (0,) * len(shape))


def on_device(frame_one, frame_two, weight, flow_grad):
    _, count, chans = frame_one.shape
    devices = lax.axis_size("pix")
    blocks = devices // 2
    frame_rows = count * devices // COLS
    scale = chans ** (-0.5)
    near = [[i for i in range(devices) if (i // 2) % 2 == z] for z in range(2)]
    across = [(i, i ^ 2) for i in range(devices)]

    one, two, grad = frame_one[0], frame_two[0], flow_grad[0]
    rows = 2 * count + 3 * GRAD_ROWS
    params = pltpu.CompilerParams(vmem_limit_bytes=48 * 1024 * 1024)
    packed = pl.pallas_call(
        pack_kernel,
        out_shape=jax.ShapeDtypeStruct((rows, chans), jnp.bfloat16),
        scratch_shapes=[pltpu.VMEM((GRAD_ROWS, LANES), jnp.float32)],
        name="pack",
    )(one, two, grad)
    with jax.named_scope("frames_across"):
        packed_far = lax.ppermute(packed, "pix", across)
    with jax.named_scope("near_gather"):
        near_both = lax.all_gather(packed, "pix", axis=0, axis_index_groups=near)
    with jax.named_scope("far_two_gather"):
        far_keys = lax.all_gather(packed_far[count : 2 * count], "pix", axis=0, axis_index_groups=near)
    with jax.named_scope("far_one_gather"):
        far_queries = lax.all_gather(packed_far, "pix", axis=0, axis_index_groups=near)

    load = chans + 3 * STAT_ROWS
    half = blocks * count
    flow, back_one, payload = pl.pallas_call(
        functools.partial(match_kernel, frame_rows, scale),
        grid=(1,),
        in_specs=[
            pl.BlockSpec((blocks, count, chans), lambda i: (0, 1, 0)),
            whole(blocks, count, chans),
            whole(count, chans),
            whole(2, count),
            whole(rows, chans),
            whole(chans, chans),
        ],
        out_specs=[whole(2, count), whole(count, chans), whole(blocks, load, LANES)],
        out_shape=[
            jax.ShapeDtypeStruct((2, count), jnp.float32),
            jax.ShapeDtypeStruct((count, chans), jnp.bfloat16),
            jax.ShapeDtypeStruct((blocks, load, LANES), jnp.bfloat16),
        ],
        scratch_shapes=[
            pltpu.VMEM((2 * half, 2 * chans), jnp.bfloat16),
            pltpu.VMEM((count, 2 * half), jnp.float32),
            pltpu.VMEM((count, 2 * half), jnp.float32),
            pltpu.VMEM((count, 2 * half), jnp.bfloat16),
            pltpu.VMEM((2 * count, chans), jnp.bfloat16),
            pltpu.VMEM((2 * count, LANES), jnp.float32),
            pltpu.VMEM((2 * count, LANES), jnp.float32),
            pltpu.VMEM((2 * count, LANES), jnp.float32),
            pltpu.VMEM((2 * count, LANES), jnp.float32),
            pltpu.VMEM((count, LANES), jnp.float32),
            pltpu.VMEM((count, LANES), jnp.float32),
            pltpu.VMEM((count, 2 * chans), jnp.float32),
            pltpu.VMEM((count, 2 * chans), jnp.bfloat16),
            pltpu.VMEM((chans, count), jnp.bfloat16),
            pltpu.VMEM((chans, count), jnp.bfloat16),
            pltpu.VMEM((LANES, 2 * count), jnp.float32),
            pltpu.VMEM((STAT_ROWS, LANES), jnp.float32),
        ],
        compiler_params=params,
        cost_estimate=pl.CostEstimate(flops=6 * 2 * count * 2 * half * chans, bytes_accessed=8 * 2**20, transcendentals=0),
        name="match",
    )(near_both, far_keys, one, grad, packed_far, weight)

    with jax.named_scope("statistics_exchange"):
        arrived = lax.all_to_all(payload, "pix", 0, 0, axis_index_groups=near)
    with jax.named_scope("weight_terms"):
        term = jnp.sum(arrived[:, 0:chans, :].astype(jnp.float32), axis=0)
        pairs = lax.axis_size("pair")
        chunk = chans // pairs
        sent = jnp.repeat(term.reshape(pairs, chunk, chans), 2, axis=0)
        planes = [
            [p * devices + z * 2 + r for p in range(pairs) for z in range(2)]
            for r in [y * 4 + c for y in range(devices // 4) for c in range(2)]
        ]
        terms = lax.all_to_all(sent, ("pair", "pix"), 0, 0, axis_index_groups=planes)
        weight_grad = jnp.sum(terms, axis=0)

    back_two = pl.pallas_call(
        functools.partial(keys_kernel, frame_rows, scale),
        grid=(1,),
        in_specs=[
            pl.BlockSpec((blocks, count, chans), lambda i: (0, 0, 0)),
            pl.BlockSpec((blocks, count, chans), lambda i: (0, 0, 0)),
            whole(blocks, load, LANES),
            whole(count, chans),
            whole(chans, chans),
        ],
        out_specs=whole(count, chans),
        out_shape=jax.ShapeDtypeStruct((count, chans), jnp.bfloat16),
        scratch_shapes=[
            pltpu.VMEM((COLS, LANES), jnp.float32),
            pltpu.VMEM((2 * half, chans), jnp.bfloat16),
            pltpu.VMEM((count, chans), jnp.bfloat16),
            pltpu.VMEM((count, count), jnp.float32),
            pltpu.VMEM((count, count), jnp.float32),
            pltpu.VMEM((count, count), jnp.bfloat16),
            pltpu.VMEM((count, count), jnp.bfloat16),
            pltpu.VMEM((count, chans), jnp.float32),
            pltpu.VMEM((blocks, STAT_ROWS, LANES), jnp.float32),
        ],
        compiler_params=params,
        cost_estimate=pl.CostEstimate(flops=6 * count * 2 * half * chans, bytes_accessed=8 * 2**20, transcendentals=0),
        name="keys",
    )(near_both, far_queries, arrived, two, weight)
    return (flow[None], back_one[None], back_two[None], weight_grad)


def solution(mesh):
    return jax.shard_map(
        on_device,
        mesh=mesh,
        in_specs=(P("pair", "pix", None), P("pair", "pix", None), P(), P("pair", None, "pix")),
        out_specs=(
            P("pair", None, "pix"),
            P("pair", "pix", None),
            P("pair", "pix", None),
            P("pair", None),
        ),
        check_vma=False,
    )
```

```python
import functools

import jax
import jax.numpy as jnp
from jax import lax
from jax.experimental import pallas as pl
from jax.experimental.pallas import tpu as pltpu
from jax.sharding import PartitionSpec as P

COLS = 128
LANES = 128
SUB = 32
GRAD_ROWS = 16
STAT_ROWS = 16
VMEM_LIMIT = 60 * 1024 * 1024
LOG2E = 1.4426950408889634


def dot(a, b, contract):
    return lax.dot_general(a, b, (contract, ((), ())), preferred_element_type=jnp.float32)


def many(low, high, each, step):
    def body(i, _):
        for k in range(each):
            step(low + i * each + k, 0)
        return 0

    lax.fori_loop(0, (high - low) // each, body, 0)


def turned(a):
    return a.astype(jnp.float32).T.astype(jnp.bfloat16)


def lane_iota(rows):
    return lax.broadcasted_iota(jnp.int32, (rows, LANES), 1)


def parted(value):
    high = value.astype(jnp.bfloat16)
    rest = value - high.astype(jnp.float32)
    middle = rest.astype(jnp.bfloat16)
    return high, middle, (rest - middle.astype(jnp.float32)).astype(jnp.bfloat16)


def joined(ref, start, rows):
    total = ref[start : start + rows, :].astype(jnp.float32)
    for part in (1, 2):
        total = total + ref[start + part * rows : start + (part + 1) * rows, :].astype(jnp.float32)
    return total


def pack_kernel(one, two, grad, first, second, spread):
    count = one.shape[0]
    wide = count // LANES
    first[0:count, :] = one[...]
    second[0:count, :] = two[...]
    second[count : count + LANES, :] = two[0:LANES, :]
    spread[...] = jnp.zeros_like(spread)
    for which in range(2):
        for j in range(wide):
            spread[which * wide + j : which * wide + j + 1, :] = grad[which : which + 1, j * LANES : (j + 1) * LANES]
    for part, value in enumerate(parted(spread[...])):
        start = count + part * GRAD_ROWS
        first[start : start + GRAD_ROWS, :] = value
    first[count + 3 * GRAD_ROWS : count + LANES, :] = jnp.zeros((LANES - 3 * GRAD_ROWS, LANES), jnp.bfloat16)


def match_kernel(
    frame_rows, scale,
    near_keys, far_keys, q_own, g_own, packed_far, weight,
    flow, back_one, payload,
    keys, score_far, score_own, prob, feat_q, grads, top, total, total_row, base, tilt, both, low, turned_q, turned_g, wide_grad, spread,
):
    blocks, count, chans = near_keys.shape[0], q_own.shape[0], q_own.shape[1]
    visits = 2 * blocks
    rows_per_block = count // COLS
    tiles = visits * rows_per_block
    unit = scale * LOG2E
    here = lax.axis_index("pix")
    z_hi = (here // 2) % 2
    w = weight[...]

    def frame_row(block, row):
        z = z_hi if block < blocks else 1 - z_hi
        place = block % blocks
        index = (place // 2) * 4 + place % 2 + 2 * z
        return (index * rows_per_block + row).astype(jnp.float32)

    feat_q[0:count, :] = dot(q_own[...], w, ((1,), (0,))).astype(jnp.bfloat16)
    feat_q[count : 2 * count, :] = dot(packed_far[0:count, :], w, ((1,), (0,))).astype(jnp.bfloat16)
    wide_grad[...] = jnp.zeros_like(wide_grad)
    wide_grad[0:2, 0:count] = g_own[...]
    far_grad = joined(packed_far, count, GRAD_ROWS)
    for which in range(2):
        for j in range(rows_per_block):
            wide_grad[which : which + 1, count + j * LANES : count + (j + 1) * LANES] = far_grad[
                which * rows_per_block + j : which * rows_per_block + j + 1, :
            ]
    grads[...] = wide_grad[...].T

    def scores(block, queries, part, score):
        start = pl.multiple_of(block * count, count)
        out = dot(queries, keys[pl.ds(start, count), 0:chans], ((1,), (1,)))
        score[:, pl.ds(start, count)] = out
        rows = slice(part * count, (part + 1) * count)
        best = top[rows, :]
        for j in range(rows_per_block):
            best = jnp.maximum(best, out[:, j * LANES : (j + 1) * LANES])
        top[rows, :] = best

    def weigh(start, size, part, score, keep):
        rows = pl.ds(start, size)
        q_rows = pl.ds(part * count + start, size)
        peak = top[q_rows, :]
        in_all = jnp.zeros((size, LANES), jnp.float32)
        in_row = jnp.zeros((size, LANES), jnp.float32)
        for j in range(tiles):
            p = jnp.exp2(score[rows, j * LANES : (j + 1) * LANES] * unit - peak)
            in_all = in_all + p
            in_row = in_row + p * frame_row(j // rows_per_block, j % rows_per_block)
            if keep:
                prob[rows, j * LANES : (j + 1) * LANES] = p.astype(jnp.bfloat16)
        total[q_rows, :] = in_all
        total_row[q_rows, :] = in_row

    def settle(part):
        rows = slice(part * count, (part + 1) * count)
        top[rows, :] = jnp.broadcast_to(jnp.max(top[rows, :], axis=1, keepdims=True) * unit, (count, LANES))

    top[...] = jnp.full_like(top, -jnp.inf)

    def first(block, _):
        start = pl.multiple_of(block * count, count)
        place = lax.rem(block, blocks)
        raw = jnp.where(block < blocks, near_keys[place], far_keys[place])
        keys[pl.ds(start, count), 0:chans] = dot(raw, w, ((1,), (0,))).astype(jnp.bfloat16)
        keys[pl.ds(start, count), chans : 2 * chans] = raw
        scores(block, feat_q[count : 2 * count, :], 1, score_far)
        return 0

    many(0, visits, 8, first)
    settle(1)

    def second(block, _):
        scores(block, feat_q[0:count, :], 0, score_own)
        size = count // visits
        weigh(pl.multiple_of(block * size, size), size, 1, score_far, False)
        return 0

    many(0, visits, 8, second)
    settle(0)

    def third(step, _):
        weigh(pl.multiple_of(step * SUB, SUB), SUB, 0, score_own, True)
        return 0

    many(0, count // SUB, 6, third)

    lane = lane_iota(2 * count)
    lane_f = lane.astype(jnp.float32)
    peak = top[:, 0:1]
    in_all = jnp.sum(total[...], axis=1, keepdims=True)
    mean_x = 2.0 * (jnp.sum(total[...] * lane_f, axis=1, keepdims=True) / in_all) / (COLS - 1) - 1.0
    mean_y = 2.0 * (jnp.sum(total_row[...], axis=1, keepdims=True) / in_all) / (frame_rows - 1) - 1.0
    grad = grads[...]
    grad_x, grad_y = grad[:, 0:1] * scale, grad[:, 1:2] * scale
    center = grad_x * mean_x + grad_y * mean_y
    level = peak + jnp.log2(in_all)
    grads[...] = jnp.where(lane == 0, level, jnp.where(lane == 1, center, jnp.where(lane == 2, mean_x, mean_y)))
    key_x = 2.0 * lane_f[0:count, :] / (COLS - 1) - 1.0
    share = 1.0 / in_all[0:count, :]
    base[...] = (grad_x[0:count, :] * key_x - center[0:count, :]) * share
    tilt[...] = jnp.broadcast_to(grad_y[0:count, :] * share, (count, LANES))
    both[...] = jnp.zeros_like(both)

    def slopes(block):
        start = pl.multiple_of(block * count, count)
        z = jnp.where(block < blocks, z_hi, 1 - z_hi)
        place = lax.rem(block, blocks)
        index = lax.div(place, 2) * 4 + lax.rem(place, 2) + 2 * z
        for j in range(rows_per_block):
            at = pl.ds(pl.multiple_of(start + j * LANES, LANES), LANES)
            key_y = 2.0 * (index * rows_per_block + j).astype(jnp.float32) / (frame_rows - 1) - 1.0
            for step in range(count // SUB):
                rows = slice(step * SUB, (step + 1) * SUB)
                value = prob[rows, at].astype(jnp.float32) * (base[rows, :] + tilt[rows, :] * key_y)
                prob[rows, at] = value.astype(jnp.bfloat16)

    def collect(block):
        start = pl.multiple_of(block * count, count)
        both[...] += dot(prob[:, pl.ds(start, count)], keys[pl.ds(start, count), :], ((1,), (0,)))

    slopes(0)

    def fourth(block, _):
        collect(block)
        slopes(block + 1)
        return 0

    many(0, visits - 1, 15, fourth)
    collect(visits - 1)
    low[...] = both[...].astype(jnp.bfloat16)
    turned_q[...] = turned(q_own[...])
    turned_g[...] = turned(low[:, chans : 2 * chans])
    back_one[...] = dot(low[:, 0:chans], w, ((1,), (1,))).astype(jnp.bfloat16)
    term = dot(turned_q[...], low[:, 0:chans], ((1,), (0,)))
    term = term + dot(turned_g[...], feat_q[0:count, :], ((1,), (0,)))

    flipped = grads[...].T
    q_lane = lax.broadcasted_iota(jnp.int32, (1, count), 1)
    q_x = 2.0 * (q_lane % COLS).astype(jnp.float32) / (COLS - 1) - 1.0
    q_y = 2.0 * (q_lane // COLS + here * rows_per_block).astype(jnp.float32) / (frame_rows - 1) - 1.0
    flow[0:1, :] = flipped[2:3, 0:count] - q_x
    flow[1:2, :] = flipped[3:4, 0:count] - q_y

    width = 2 * count // LANES
    payload[0, 0:chans, :] = term.astype(jnp.bfloat16)
    spread[...] = jnp.zeros_like(spread)
    for which in range(2):
        for j in range(width):
            spread[which * width + j : which * width + j + 1, :] = flipped[which : which + 1, j * LANES : (j + 1) * LANES]
    for part, value in enumerate(parted(spread[...])):
        payload[0, chans + part * STAT_ROWS : chans + (part + 1) * STAT_ROWS, :] = value

    def copies(device, _):
        payload[device] = payload[0]
        return 0

    lax.fori_loop(1, blocks, copies, 0)


def keys_kernel(
    frame_rows, scale,
    near_q, far_q, arrived, frame_two, weight,
    back_two,
    column, feat_q, feat_k, score_a, score_b, slope_a, slope_b, acc, stat,
):
    blocks, chans = near_q.shape[0], near_q.shape[2]
    count = frame_two.shape[0]
    unit = scale * LOG2E
    here = lax.axis_index("pix")
    rows_per_block = count // COLS
    width = 2 * count // LANES
    w = weight[...]
    feat_k[...] = dot(frame_two[...], w, ((1,), (0,))).astype(jnp.bfloat16)
    sub = lax.broadcasted_iota(jnp.int32, (COLS, LANES), 0)
    column[...] = 2.0 * sub.astype(jnp.float32) / (COLS - 1) - 1.0
    tiles = count // LANES
    acc[...] = jnp.zeros_like(acc)
    for block in range(blocks):
        stat[block, 0:STAT_ROWS, :] = joined(arrived.at[block], chans, STAT_ROWS)
        for part, source in ((0, near_q), (1, far_q)):
            start = STAT_ROWS + part * GRAD_ROWS
            stat[block, start : start + GRAD_ROWS, :] = joined(source.at[block], count, GRAD_ROWS) * scale

    def project(block, _):
        for part, source in ((0, near_q), (1, far_q)):
            start = pl.multiple_of((block * 2 + part) * count, count)
            feat_q[pl.ds(start, count), :] = dot(source[block, 0:count, :], w, ((1,), (0,))).astype(jnp.bfloat16)
        return 0

    many(0, blocks, 4, project)

    def queries(visit):
        return feat_q[pl.ds(pl.multiple_of(visit * count, count), count), :]

    def scores(visit, score):
        score[...] = dot(feat_k[...], queries(visit), ((1,), (1,)))

    def slopes(block, part, score, slope):
        for j in range(tiles):
            at = part * tiles + j
            level = stat[block, at : at + 1, :]
            center = stat[block, width + at : width + at + 1, :]
            grad_at = STAT_ROWS + part * GRAD_ROWS + j
            grad_x = stat[block, grad_at : grad_at + 1, :]
            grad_y = stat[block, grad_at + tiles : grad_at + tiles + 1, :]
            for row in range(rows_per_block):
                key_y = 2.0 * (here * rows_per_block + row).astype(jnp.float32) / (frame_rows - 1) - 1.0
                offset = grad_y * key_y - center
                for step in range(COLS // SUB):
                    rows = slice(row * COLS + step * SUB, row * COLS + (step + 1) * SUB)
                    p = jnp.exp2(score[rows, j * LANES : (j + 1) * LANES] * unit - level)
                    value = p * (column[step * SUB : (step + 1) * SUB, :] * grad_x + offset)
                    slope[rows, j * LANES : (j + 1) * LANES] = value.astype(jnp.bfloat16)

    def collect(visit, slope):
        acc[...] += dot(slope[...], queries(visit), ((1,), (0,)))

    scores(0, score_a)
    slope_b[...] = jnp.zeros_like(slope_b)

    def visit(block, _):
        first, second = 2 * block, 2 * block + 1
        scores(second, score_b)
        slopes(block, 0, score_a, slope_a)
        collect(jnp.maximum(second - 2, 0), slope_b)
        scores(jnp.minimum(first + 2, 2 * blocks - 1), score_a)
        slopes(block, 1, score_b, slope_b)
        collect(first, slope_a)
        return 0

    many(0, blocks, 4, visit)
    collect(2 * blocks - 1, slope_b)
    back_two[...] = dot(acc[...].astype(jnp.bfloat16), w, ((1,), (1,))).astype(jnp.bfloat16)


def whole(*shape):
    return pl.BlockSpec(shape, lambda i: (0,) * len(shape))


def on_device(frame_one, frame_two, weight, flow_grad):
    _, count, chans = frame_one.shape
    devices = lax.axis_size("pix")
    blocks = devices // 2
    frame_rows = count * devices // COLS
    scale = chans ** (-0.5)
    near = [[i for i in range(devices) if (i // 2) % 2 == z] for z in range(2)]
    across = [(i, i ^ 2) for i in range(devices)]

    one, two, grad = frame_one[0], frame_two[0], flow_grad[0]
    rows = count + LANES
    params = pltpu.CompilerParams(vmem_limit_bytes=VMEM_LIMIT)
    packed_one, packed_two = pl.pallas_call(
        pack_kernel,
        out_shape=[jax.ShapeDtypeStruct((rows, chans), jnp.bfloat16)] * 2,
        scratch_shapes=[pltpu.VMEM((GRAD_ROWS, LANES), jnp.float32)],
        name="pack",
    )(one, two, grad)
    with jax.named_scope("frame_two_across"):
        far_two = lax.ppermute(two, "pix", across)
    with jax.named_scope("frame_one_across"):
        packed_far = lax.ppermute(packed_one, "pix", across)
    with jax.named_scope("near_two_gather"):
        near_keys = lax.all_gather(packed_two, "pix", axis=0, axis_index_groups=near)
    with jax.named_scope("near_one_gather"):
        near_queries = lax.all_gather(packed_one, "pix", axis=0, axis_index_groups=near)
    with jax.named_scope("far_two_gather"):
        far_keys = lax.all_gather(far_two, "pix", axis=0, axis_index_groups=near)
    with jax.named_scope("far_one_gather"):
        later_far, far_keys = lax.optimization_barrier((packed_far, far_keys))
        far_queries = lax.all_gather(later_far, "pix", axis=0, axis_index_groups=near)

    load = chans + 3 * STAT_ROWS
    pairs = lax.axis_size("pair")
    chunk = chans // pairs
    half = blocks * count
    flow, back_one, payload = pl.pallas_call(
        functools.partial(match_kernel, frame_rows, scale),
        grid=(1,),
        in_specs=[
            pl.BlockSpec((blocks, count, chans), lambda i: (0, 0, 0)),
            whole(blocks, count, chans),
            whole(count, chans),
            whole(2, count),
            whole(rows, chans),
            whole(chans, chans),
        ],
        out_specs=[whole(2, count), whole(count, chans), whole(blocks, load, LANES)],
        out_shape=[
            jax.ShapeDtypeStruct((2, count), jnp.float32),
            jax.ShapeDtypeStruct((count, chans), jnp.bfloat16),
            jax.ShapeDtypeStruct((blocks, load, LANES), jnp.bfloat16),
        ],
        scratch_shapes=[
            pltpu.VMEM((2 * half, 2 * chans), jnp.bfloat16),
            pltpu.VMEM((count, 2 * half), jnp.float32),
            pltpu.VMEM((count, 2 * half), jnp.float32),
            pltpu.VMEM((count, 2 * half), jnp.bfloat16),
            pltpu.VMEM((2 * count, chans), jnp.bfloat16),
            pltpu.VMEM((2 * count, LANES), jnp.float32),
            pltpu.VMEM((2 * count, LANES), jnp.float32),
            pltpu.VMEM((2 * count, LANES), jnp.float32),
            pltpu.VMEM((2 * count, LANES), jnp.float32),
            pltpu.VMEM((count, LANES), jnp.float32),
            pltpu.VMEM((count, LANES), jnp.float32),
            pltpu.VMEM((count, 2 * chans), jnp.float32),
            pltpu.VMEM((count, 2 * chans), jnp.bfloat16),
            pltpu.VMEM((chans, count), jnp.bfloat16),
            pltpu.VMEM((chans, count), jnp.bfloat16),
            pltpu.VMEM((LANES, 2 * count), jnp.float32),
            pltpu.VMEM((STAT_ROWS, LANES), jnp.float32),
        ],
        compiler_params=params,
        cost_estimate=pl.CostEstimate(flops=6 * 2 * count * 2 * half * chans, bytes_accessed=8 * 2**20, transcendentals=0),
        name="match",
    )(near_keys, far_keys, one, grad, packed_far, weight)

    with jax.named_scope("statistics_exchange"):
        arrived = lax.all_to_all(payload, "pix", 0, 0, axis_index_groups=near)
    with jax.named_scope("weight_terms"):
        term = jnp.sum(arrived[:, 0:chans, :].astype(jnp.float32), axis=0)
        sent = jnp.repeat(term.reshape(pairs, chunk, chans), 2, axis=0)
        planes = [
            [p * devices + z * 2 + r for p in range(pairs) for z in range(2)]
            for r in [y * 4 + c for y in range(devices // 4) for c in range(2)]
        ]
        terms = lax.all_to_all(sent, ("pair", "pix"), 0, 0, axis_index_groups=planes)
        weight_grad = jnp.sum(terms, axis=0)
    back_two = pl.pallas_call(
        functools.partial(keys_kernel, frame_rows, scale),
        grid=(1,),
        in_specs=[
            whole(blocks, rows, chans),
            whole(blocks, rows, chans),
            whole(blocks, load, LANES),
            whole(count, chans),
            whole(chans, chans),
        ],
        out_specs=whole(count, chans),
        out_shape=jax.ShapeDtypeStruct((count, chans), jnp.bfloat16),
        scratch_shapes=[
            pltpu.VMEM((COLS, LANES), jnp.float32),
            pltpu.VMEM((2 * half, chans), jnp.bfloat16),
            pltpu.VMEM((count, chans), jnp.bfloat16),
            pltpu.VMEM((count, count), jnp.float32),
            pltpu.VMEM((count, count), jnp.float32),
            pltpu.VMEM((count, count), jnp.bfloat16),
            pltpu.VMEM((count, count), jnp.bfloat16),
            pltpu.VMEM((count, chans), jnp.float32),
            pltpu.VMEM((blocks, STAT_ROWS + 2 * GRAD_ROWS, LANES), jnp.float32),
        ],
        compiler_params=params,
        cost_estimate=pl.CostEstimate(flops=6 * count * 2 * half * chans, bytes_accessed=8 * 2**20, transcendentals=0),
        name="keys",
    )(near_queries, far_queries, arrived, two, weight)
    return (flow[None], back_one[None], back_two[None], weight_grad)


def solution(mesh):
    return jax.shard_map(
        on_device,
        mesh=mesh,
        in_specs=(P("pair", "pix", None), P("pair", "pix", None), P(), P("pair", None, "pix")),
        out_specs=(
            P("pair", None, "pix"),
            P("pair", "pix", None),
            P("pair", "pix", None),
            P("pair", None),
        ),
        check_vma=False,
    )
```

```python
import functools

import jax
import jax.numpy as jnp
from jax import lax
from jax.experimental import pallas as pl
from jax.experimental.pallas import tpu as pltpu
from jax.sharding import PartitionSpec as P

COLS = 128
LANES = 128
SUB = 32
FIRST = 4
SECOND = 4
THIRD = 6
GRAD_ROWS = 16
STAT_ROWS = 16
VMEM_LIMIT = 60 * 1024 * 1024
LOG2E = 1.4426950408889634


def dot(a, b, contract):
    return lax.dot_general(a, b, (contract, ((), ())), preferred_element_type=jnp.float32)


def many(low, high, each, step):
    def body(i, _):
        for k in range(each):
            step(low + i * each + k, 0)
        return 0

    lax.fori_loop(0, (high - low) // each, body, 0)


def turned(a):
    return a.astype(jnp.float32).T.astype(jnp.bfloat16)


def lane_iota(rows):
    return lax.broadcasted_iota(jnp.int32, (rows, LANES), 1)


def parted(value):
    high = value.astype(jnp.bfloat16)
    rest = value - high.astype(jnp.float32)
    middle = rest.astype(jnp.bfloat16)
    return high, middle, (rest - middle.astype(jnp.float32)).astype(jnp.bfloat16)


def joined(ref, start, rows):
    total = ref[start : start + rows, :].astype(jnp.float32)
    for part in (1, 2):
        total = total + ref[start + part * rows : start + (part + 1) * rows, :].astype(jnp.float32)
    return total


def pack_kernel(one, two, grad, both, first, spread):
    count = one.shape[0]
    wide = count // LANES
    both[0:count, :] = two[...]
    both[count : 2 * count, :] = one[...]
    first[0:count, :] = one[...]
    spread[...] = jnp.zeros_like(spread)
    for which in range(2):
        for j in range(wide):
            spread[which * wide + j : which * wide + j + 1, :] = grad[which : which + 1, j * LANES : (j + 1) * LANES]
    for part, value in enumerate(parted(spread[...])):
        start = count + part * GRAD_ROWS
        first[start : start + GRAD_ROWS, :] = value
        both[count + start : count + start + GRAD_ROWS, :] = value
    first[count + 3 * GRAD_ROWS : count + LANES, :] = jnp.zeros((LANES - 3 * GRAD_ROWS, LANES), jnp.bfloat16)


def match_kernel(
    frame_rows, scale,
    near_keys, far_keys, q_own, g_own, packed_far, weight,
    flow, back_one, payload,
    keys, score_far, score_own, prob, feat_q, grads, top, total, total_row, base, tilt, both, low, turned_q, turned_g, wide_grad, spread,
):
    blocks, count, chans = near_keys.shape[0], q_own.shape[0], q_own.shape[1]
    span = 2 * count
    visits = blocks
    rows_per_block = count // COLS
    tiles = 2 * blocks * rows_per_block
    unit = scale * LOG2E
    here = lax.axis_index("pix")
    z_hi = (here // 2) % 2
    w = weight[...]

    def frame_row(block, row):
        z = z_hi if block < blocks else 1 - z_hi
        place = block % blocks
        index = (place // 2) * 4 + place % 2 + 2 * z
        return (index * rows_per_block + row).astype(jnp.float32)

    feat_q[0:count, :] = dot(q_own[...], w, ((1,), (0,))).astype(jnp.bfloat16)
    feat_q[count : 2 * count, :] = dot(packed_far[0:count, :], w, ((1,), (0,))).astype(jnp.bfloat16)
    wide_grad[...] = jnp.zeros_like(wide_grad)
    wide_grad[0:2, 0:count] = g_own[...]
    far_grad = joined(packed_far, count, GRAD_ROWS)
    for which in range(2):
        for j in range(rows_per_block):
            wide_grad[which : which + 1, count + j * LANES : count + (j + 1) * LANES] = far_grad[
                which * rows_per_block + j : which * rows_per_block + j + 1, :
            ]
    grads[...] = wide_grad[...].T

    def scores(visit, queries, part, score):
        start = pl.multiple_of(visit * span, span)
        out = dot(queries, keys[pl.ds(start, span), 0:chans], ((1,), (1,)))
        score[:, pl.ds(start, span)] = out
        rows = slice(part * count, (part + 1) * count)
        best = top[rows, :]
        for j in range(span // LANES):
            best = jnp.maximum(best, out[:, j * LANES : (j + 1) * LANES])
        top[rows, :] = best

    def weigh(start, size, part, score, keep):
        rows = pl.ds(start, size)
        q_rows = pl.ds(part * count + start, size)
        peak = top[q_rows, :]
        in_all = jnp.zeros((size, LANES), jnp.float32)
        in_row = jnp.zeros((size, LANES), jnp.float32)
        for j in range(tiles):
            p = jnp.exp2(score[rows, j * LANES : (j + 1) * LANES] * unit - peak)
            in_all = in_all + p
            in_row = in_row + p * frame_row(j // rows_per_block, j % rows_per_block)
            if keep:
                prob[rows, j * LANES : (j + 1) * LANES] = p.astype(jnp.bfloat16)
        total[q_rows, :] = in_all
        total_row[q_rows, :] = in_row

    def settle(part):
        rows = slice(part * count, (part + 1) * count)
        top[rows, :] = jnp.broadcast_to(jnp.max(top[rows, :], axis=1, keepdims=True) * unit, (count, LANES))

    top[...] = jnp.full_like(top, -jnp.inf)

    def first(visit, source, begin):
        for half in range(2):
            start = pl.multiple_of((begin + visit) * span + half * count, count)
            raw = source[2 * visit + half]
            keys[pl.ds(start, count), 0:chans] = dot(raw, w, ((1,), (0,))).astype(jnp.bfloat16)
            keys[pl.ds(start, count), chans : 2 * chans] = raw
        scores(begin + visit, feat_q[count : 2 * count, :], 1, score_far)

    many(0, visits // 2, FIRST, lambda visit, _: first(visit, near_keys, 0))
    many(0, visits // 2, FIRST, lambda visit, _: first(visit, far_keys, visits // 2))
    settle(1)

    def second(block, _):
        scores(block, feat_q[0:count, :], 0, score_own)
        size = count // visits
        weigh(pl.multiple_of(block * size, size), size, 1, score_far, False)
        return 0

    many(0, visits, SECOND, second)
    settle(0)

    def third(step, _):
        weigh(pl.multiple_of(step * SUB, SUB), SUB, 0, score_own, True)
        return 0

    many(0, count // SUB, THIRD, third)

    lane = lane_iota(2 * count)
    lane_f = lane.astype(jnp.float32)
    peak = top[:, 0:1]
    in_all = jnp.sum(total[...], axis=1, keepdims=True)
    mean_x = 2.0 * (jnp.sum(total[...] * lane_f, axis=1, keepdims=True) / in_all) / (COLS - 1) - 1.0
    mean_y = 2.0 * (jnp.sum(total_row[...], axis=1, keepdims=True) / in_all) / (frame_rows - 1) - 1.0
    grad = grads[...]
    grad_x, grad_y = grad[:, 0:1] * scale, grad[:, 1:2] * scale
    center = grad_x * mean_x + grad_y * mean_y
    level = peak + jnp.log2(in_all)
    grads[...] = jnp.where(lane == 0, level, jnp.where(lane == 1, center, jnp.where(lane == 2, mean_x, mean_y)))
    key_x = 2.0 * lane_f[0:count, :] / (COLS - 1) - 1.0
    share = 1.0 / in_all[0:count, :]
    base[...] = (grad_x[0:count, :] * key_x - center[0:count, :]) * share
    tilt[...] = jnp.broadcast_to(grad_y[0:count, :] * share, (count, LANES))
    both[...] = jnp.zeros_like(both)

    def slopes(visit):
        z = jnp.where(visit < visits // 2, z_hi, 1 - z_hi)
        place = lax.rem(visit, visits // 2)
        for j in range(span // LANES):
            at = pl.ds(pl.multiple_of(visit * span + j * LANES, LANES), LANES)
            index = place * 4 + j // rows_per_block + 2 * z
            key_y = 2.0 * (index * rows_per_block + j % rows_per_block).astype(jnp.float32) / (frame_rows - 1) - 1.0
            for step in range(count // SUB):
                rows = slice(step * SUB, (step + 1) * SUB)
                value = prob[rows, at].astype(jnp.float32) * (base[rows, :] + tilt[rows, :] * key_y)
                prob[rows, at] = value.astype(jnp.bfloat16)

    def collect(visit):
        start = pl.multiple_of(visit * span, span)
        both[...] += dot(prob[:, pl.ds(start, span)], keys[pl.ds(start, span), :], ((1,), (0,)))

    slopes(0)

    def fourth(block, _):
        collect(block)
        slopes(block + 1)
        return 0

    many(0, visits - 1, 7, fourth)
    collect(visits - 1)
    low[...] = both[...].astype(jnp.bfloat16)
    turned_q[...] = turned(q_own[...])
    turned_g[...] = turned(low[:, chans : 2 * chans])
    back_one[...] = dot(low[:, 0:chans], w, ((1,), (1,))).astype(jnp.bfloat16)
    term = dot(turned_q[...], low[:, 0:chans], ((1,), (0,)))
    term = term + dot(turned_g[...], feat_q[0:count, :], ((1,), (0,)))

    flipped = grads[...].T
    q_lane = lax.broadcasted_iota(jnp.int32, (1, count), 1)
    q_x = 2.0 * (q_lane % COLS).astype(jnp.float32) / (COLS - 1) - 1.0
    q_y = 2.0 * (q_lane // COLS + here * rows_per_block).astype(jnp.float32) / (frame_rows - 1) - 1.0
    flow[0:1, :] = flipped[2:3, 0:count] - q_x
    flow[1:2, :] = flipped[3:4, 0:count] - q_y

    width = 2 * count // LANES
    payload[0, 0:chans, :] = term.astype(jnp.bfloat16)
    spread[...] = jnp.zeros_like(spread)
    for which in range(2):
        for j in range(width):
            spread[which * width + j : which * width + j + 1, :] = flipped[which : which + 1, j * LANES : (j + 1) * LANES]
    for part, value in enumerate(parted(spread[...])):
        payload[0, chans + part * STAT_ROWS : chans + (part + 1) * STAT_ROWS, :] = value

    def copies(device, _):
        payload[device] = payload[0]
        return 0

    lax.fori_loop(1, blocks, copies, 0)


def keys_kernel(
    frame_rows, scale,
    near_q, far_q, arrived, frame_two, weight,
    back_two,
    column, feat_q, feat_k, score_a, score_b, slope_a, slope_b, acc, stat,
):
    blocks, chans = near_q.shape[0], near_q.shape[2]
    count = frame_two.shape[0]
    unit = scale * LOG2E
    here = lax.axis_index("pix")
    rows_per_block = count // COLS
    width = 2 * count // LANES
    w = weight[...]
    feat_k[...] = dot(frame_two[...], w, ((1,), (0,))).astype(jnp.bfloat16)
    sub = lax.broadcasted_iota(jnp.int32, (COLS, LANES), 0)
    column[...] = 2.0 * sub.astype(jnp.float32) / (COLS - 1) - 1.0
    tiles = count // LANES
    acc[...] = jnp.zeros_like(acc)
    for block in range(blocks):
        stat[block, 0:STAT_ROWS, :] = joined(arrived.at[block], chans, STAT_ROWS)
        for part, source, first in ((0, near_q, count), (1, far_q, 0)):
            start = STAT_ROWS + part * GRAD_ROWS
            stat[block, start : start + GRAD_ROWS, :] = joined(source.at[block], first + count, GRAD_ROWS) * scale

    def project(block, _):
        for part, source, first in ((0, near_q, count), (1, far_q, 0)):
            start = pl.multiple_of((block * 2 + part) * count, count)
            feat_q[pl.ds(start, count), :] = dot(source[block, first : first + count, :], w, ((1,), (0,))).astype(jnp.bfloat16)
        return 0

    many(0, blocks, 4, project)

    def queries(visit):
        return feat_q[pl.ds(pl.multiple_of(visit * count, count), count), :]

    def scores(visit, score):
        score[...] = dot(feat_k[...], queries(visit), ((1,), (1,)))

    def slopes(block, part, score, slope):
        for j in range(tiles):
            at = part * tiles + j
            level = stat[block, at : at + 1, :]
            center = stat[block, width + at : width + at + 1, :]
            grad_at = STAT_ROWS + part * GRAD_ROWS + j
            grad_x = stat[block, grad_at : grad_at + 1, :]
            grad_y = stat[block, grad_at + tiles : grad_at + tiles + 1, :]
            for row in range(rows_per_block):
                key_y = 2.0 * (here * rows_per_block + row).astype(jnp.float32) / (frame_rows - 1) - 1.0
                offset = grad_y * key_y - center
                for step in range(COLS // SUB):
                    rows = slice(row * COLS + step * SUB, row * COLS + (step + 1) * SUB)
                    p = jnp.exp2(score[rows, j * LANES : (j + 1) * LANES] * unit - level)
                    value = p * (column[step * SUB : (step + 1) * SUB, :] * grad_x + offset)
                    slope[rows, j * LANES : (j + 1) * LANES] = value.astype(jnp.bfloat16)

    def collect(visit, slope):
        acc[...] += dot(slope[...], queries(visit), ((1,), (0,)))

    scores(0, score_a)
    slope_b[...] = jnp.zeros_like(slope_b)

    def visit(block, _):
        first, second = 2 * block, 2 * block + 1
        scores(second, score_b)
        slopes(block, 0, score_a, slope_a)
        collect(jnp.maximum(second - 2, 0), slope_b)
        scores(jnp.minimum(first + 2, 2 * blocks - 1), score_a)
        slopes(block, 1, score_b, slope_b)
        collect(first, slope_a)
        return 0

    many(0, blocks, 4, visit)
    collect(2 * blocks - 1, slope_b)
    back_two[...] = dot(acc[...].astype(jnp.bfloat16), w, ((1,), (1,))).astype(jnp.bfloat16)


def whole(*shape):
    return pl.BlockSpec(shape, lambda i: (0,) * len(shape))


def on_device(frame_one, frame_two, weight, flow_grad):
    _, count, chans = frame_one.shape
    devices = lax.axis_size("pix")
    blocks = devices // 2
    frame_rows = count * devices // COLS
    scale = chans ** (-0.5)
    near = [[i for i in range(devices) if (i // 2) % 2 == z] for z in range(2)]
    across = [(i, i ^ 2) for i in range(devices)]

    one, two, grad = frame_one[0], frame_two[0], flow_grad[0]
    rows = count + LANES
    params = pltpu.CompilerParams(vmem_limit_bytes=VMEM_LIMIT)
    near_rows = 2 * count + 3 * GRAD_ROWS
    packed_both, packed_one = pl.pallas_call(
        pack_kernel,
        out_shape=[
            jax.ShapeDtypeStruct((near_rows, chans), jnp.bfloat16),
            jax.ShapeDtypeStruct((rows, chans), jnp.bfloat16),
        ],
        scratch_shapes=[pltpu.VMEM((GRAD_ROWS, LANES), jnp.float32)],
        name="pack",
    )(one, two, grad)
    with jax.named_scope("frame_two_across"):
        far_two = lax.ppermute(two, "pix", across)
    with jax.named_scope("frame_one_across"):
        packed_far = lax.ppermute(packed_one, "pix", across)
    with jax.named_scope("near_gather"):
        near_both = lax.all_gather(packed_both, "pix", axis=0, axis_index_groups=near)
    with jax.named_scope("far_two_gather"):
        far_keys = lax.all_gather(far_two, "pix", axis=0, axis_index_groups=near)
    with jax.named_scope("far_one_gather"):
        later_far, far_keys = lax.optimization_barrier((packed_far, far_keys))
        far_queries = lax.all_gather(later_far, "pix", axis=0, axis_index_groups=near)

    load = chans + 3 * STAT_ROWS
    pairs = lax.axis_size("pair")
    chunk = chans // pairs
    half = blocks * count
    flow, back_one, payload = pl.pallas_call(
        functools.partial(match_kernel, frame_rows, scale),
        grid=(1,),
        in_specs=[
            pl.BlockSpec((blocks, count, chans), lambda i: (0, 0, 0)),
            whole(blocks, count, chans),
            whole(count, chans),
            whole(2, count),
            whole(rows, chans),
            whole(chans, chans),
        ],
        out_specs=[whole(2, count), whole(count, chans), whole(blocks, load, LANES)],
        out_shape=[
            jax.ShapeDtypeStruct((2, count), jnp.float32),
            jax.ShapeDtypeStruct((count, chans), jnp.bfloat16),
            jax.ShapeDtypeStruct((blocks, load, LANES), jnp.bfloat16),
        ],
        scratch_shapes=[
            pltpu.VMEM((2 * half, 2 * chans), jnp.bfloat16),
            pltpu.VMEM((count, 2 * half), jnp.float32),
            pltpu.VMEM((count, 2 * half), jnp.float32),
            pltpu.VMEM((count, 2 * half), jnp.bfloat16),
            pltpu.VMEM((2 * count, chans), jnp.bfloat16),
            pltpu.VMEM((2 * count, LANES), jnp.float32),
            pltpu.VMEM((2 * count, LANES), jnp.float32),
            pltpu.VMEM((2 * count, LANES), jnp.float32),
            pltpu.VMEM((2 * count, LANES), jnp.float32),
            pltpu.VMEM((count, LANES), jnp.float32),
            pltpu.VMEM((count, LANES), jnp.float32),
            pltpu.VMEM((count, 2 * chans), jnp.float32),
            pltpu.VMEM((count, 2 * chans), jnp.bfloat16),
            pltpu.VMEM((chans, count), jnp.bfloat16),
            pltpu.VMEM((chans, count), jnp.bfloat16),
            pltpu.VMEM((LANES, 2 * count), jnp.float32),
            pltpu.VMEM((STAT_ROWS, LANES), jnp.float32),
        ],
        compiler_params=params,
        cost_estimate=pl.CostEstimate(flops=6 * 2 * count * 2 * half * chans, bytes_accessed=8 * 2**20, transcendentals=0),
        name="match",
    )(near_both, far_keys, one, grad, packed_far, weight)

    with jax.named_scope("statistics_exchange"):
        arrived = lax.all_to_all(payload, "pix", 0, 0, axis_index_groups=near)
    with jax.named_scope("weight_terms"):
        term = jnp.sum(arrived[:, 0:chans, :].astype(jnp.float32), axis=0).astype(jnp.bfloat16)
        sent = jnp.repeat(term.reshape(pairs, chunk, chans), 2, axis=0)
        planes = [
            [p * devices + z * 2 + r for p in range(pairs) for z in range(2)]
            for r in [y * 4 + c for y in range(devices // 4) for c in range(2)]
        ]
        terms = lax.all_to_all(sent, ("pair", "pix"), 0, 0, axis_index_groups=planes)
        weight_grad = jnp.sum(terms.astype(jnp.float32), axis=0)
    back_two = pl.pallas_call(
        functools.partial(keys_kernel, frame_rows, scale),
        grid=(1,),
        in_specs=[
            whole(blocks, near_rows, chans),
            whole(blocks, rows, chans),
            whole(blocks, load, LANES),
            whole(count, chans),
            whole(chans, chans),
        ],
        out_specs=whole(count, chans),
        out_shape=jax.ShapeDtypeStruct((count, chans), jnp.bfloat16),
        scratch_shapes=[
            pltpu.VMEM((COLS, LANES), jnp.float32),
            pltpu.VMEM((2 * half, chans), jnp.bfloat16),
            pltpu.VMEM((count, chans), jnp.bfloat16),
            pltpu.VMEM((count, count), jnp.float32),
            pltpu.VMEM((count, count), jnp.float32),
            pltpu.VMEM((count, count), jnp.bfloat16),
            pltpu.VMEM((count, count), jnp.bfloat16),
            pltpu.VMEM((count, chans), jnp.float32),
            pltpu.VMEM((blocks, STAT_ROWS + 2 * GRAD_ROWS, LANES), jnp.float32),
        ],
        compiler_params=params,
        cost_estimate=pl.CostEstimate(flops=6 * count * 2 * half * chans, bytes_accessed=8 * 2**20, transcendentals=0),
        name="keys",
    )(near_both, far_queries, arrived, two, weight)
    return (flow[None], back_one[None], back_two[None], weight_grad)


def solution(mesh):
    return jax.shard_map(
        on_device,
        mesh=mesh,
        in_specs=(P("pair", "pix", None), P("pair", "pix", None), P(), P("pair", None, "pix")),
        out_specs=(
            P("pair", None, "pix"),
            P("pair", "pix", None),
            P("pair", "pix", None),
            P("pair", None),
        ),
        check_vma=False,
    )
```

```python
import functools

import jax
import jax.numpy as jnp
from jax import lax
from jax.experimental import pallas as pl
from jax.experimental.pallas import tpu as pltpu
from jax.sharding import PartitionSpec as P

COLS = 128
LANES = 128
SUB = 32
FIRST = 4
SECOND = 4
THIRD = 6
GRAD_ROWS = 16
VMEM_LIMIT = 60 * 1024 * 1024
LOG2E = 1.4426950408889634


def dot(a, b, contract):
    return lax.dot_general(a, b, (contract, ((), ())), preferred_element_type=jnp.float32)


def many(low, high, each, step):
    def body(i, _):
        for k in range(each):
            step(low + i * each + k, 0)
        return 0

    lax.fori_loop(0, (high - low) // each, body, 0)


def turned(a):
    return a.astype(jnp.float32).T.astype(jnp.bfloat16)


def lane_iota(rows):
    return lax.broadcasted_iota(jnp.int32, (rows, LANES), 1)


def parted(value):
    high = value.astype(jnp.bfloat16)
    rest = value - high.astype(jnp.float32)
    middle = rest.astype(jnp.bfloat16)
    return high, middle, (rest - middle.astype(jnp.float32)).astype(jnp.bfloat16)


def joined(ref, start, rows):
    total = ref[start : start + rows, :].astype(jnp.float32)
    for part in (1, 2):
        total = total + ref[start + part * rows : start + (part + 1) * rows, :].astype(jnp.float32)
    return total


def pack_kernel(one, grad, out, spread):
    count = one.shape[0]
    wide = count // LANES
    out[0:count, :] = one[...]
    spread[...] = jnp.zeros_like(spread)
    for which in range(2):
        for j in range(wide):
            spread[which * wide + j : which * wide + j + 1, :] = grad[which : which + 1, j * LANES : (j + 1) * LANES]
    for part, value in enumerate(parted(spread[...])):
        start = count + part * GRAD_ROWS
        out[start : start + GRAD_ROWS, :] = value


def match_kernel(
    frame_rows, scale,
    near_keys, far_keys, q_own, g_own, packed_far, weight,
    flow, back_one, payload,
    keys, score_far, score_own, prob, prob_far, feat_q, feat_turned, grads, top, total, total_row, base, tilt, both, low, turned_q, turned_g, wide_grad,
):
    blocks, count, chans = near_keys.shape[0], q_own.shape[0], q_own.shape[1]
    span = 2 * count
    visits = blocks
    rows_per_block = count // COLS
    tiles = 2 * blocks * rows_per_block
    unit = scale * LOG2E
    here = lax.axis_index("pix")
    z_hi = (here // 2) % 2
    w = weight[...]

    def frame_row(block, row):
        z = z_hi if block < blocks else 1 - z_hi
        place = block % blocks
        index = (place // 2) * 4 + place % 2 + 2 * z
        return (index * rows_per_block + row).astype(jnp.float32)

    feat_q[0:count, :] = dot(q_own[...], w, ((1,), (0,))).astype(jnp.bfloat16)
    feat_q[count : 2 * count, :] = dot(packed_far[0:count, :], w, ((1,), (0,))).astype(jnp.bfloat16)
    feat_turned[...] = turned(feat_q[...])
    wide_grad[...] = jnp.zeros_like(wide_grad)
    wide_grad[0:2, 0:count] = g_own[...]
    far_grad = joined(packed_far, count, GRAD_ROWS)
    for which in range(2):
        for j in range(rows_per_block):
            wide_grad[which : which + 1, count + j * LANES : count + (j + 1) * LANES] = far_grad[
                which * rows_per_block + j : which * rows_per_block + j + 1, :
            ]
    grads[...] = wide_grad[...].T

    def scores(visit, queries, part, score):
        start = pl.multiple_of(visit * span, span)
        out = dot(queries, keys[pl.ds(start, span), 0:chans], ((1,), (1,)))
        score[:, pl.ds(start, span)] = out
        rows = slice(part * count, (part + 1) * count)
        best = top[rows, :]
        for j in range(span // LANES):
            best = jnp.maximum(best, out[:, j * LANES : (j + 1) * LANES])
        top[rows, :] = best

    def weigh(start, size, part, score, kept, keep):
        rows = pl.ds(start, size)
        q_rows = pl.ds(part * count + start, size)
        peak = top[q_rows, :]
        in_all = jnp.zeros((size, LANES), jnp.float32)
        in_row = jnp.zeros((size, LANES), jnp.float32)
        for j in range(tiles):
            p = jnp.exp2(score[rows, j * LANES : (j + 1) * LANES] * unit - peak)
            in_all = in_all + p
            in_row = in_row + p * frame_row(j // rows_per_block, j % rows_per_block)
            if j < keep:
                kept[rows, j * LANES : (j + 1) * LANES] = p.astype(jnp.bfloat16)
        total[q_rows, :] = in_all
        total_row[q_rows, :] = in_row

    def settle(part):
        rows = slice(part * count, (part + 1) * count)
        top[rows, :] = jnp.broadcast_to(jnp.max(top[rows, :], axis=1, keepdims=True) * unit, (count, LANES))

    top[...] = jnp.full_like(top, -jnp.inf)

    def first(visit, source, begin):
        for half in range(2):
            start = pl.multiple_of((begin + visit) * span + half * count, count)
            raw = source[2 * visit + half]
            keys[pl.ds(start, count), 0:chans] = dot(raw, w, ((1,), (0,))).astype(jnp.bfloat16)
            keys[pl.ds(start, count), chans : 2 * chans] = raw
        scores(begin + visit, feat_q[count : 2 * count, :], 1, score_far)

    many(0, visits // 2, FIRST, lambda visit, _: first(visit, near_keys, 0))
    many(0, visits // 2, FIRST, lambda visit, _: first(visit, far_keys, visits // 2))
    settle(1)

    def second(block, _):
        scores(block, feat_q[0:count, :], 0, score_own)
        size = count // visits
        weigh(pl.multiple_of(block * size, size), size, 1, score_far, prob_far, tiles // 2)
        return 0

    many(0, visits, SECOND, second)
    settle(0)

    def third(step, _):
        weigh(pl.multiple_of(step * SUB, SUB), SUB, 0, score_own, prob, tiles)
        return 0

    many(0, count // SUB, THIRD, third)

    lane = lane_iota(2 * count)
    lane_f = lane.astype(jnp.float32)
    in_all = jnp.sum(total[...], axis=1, keepdims=True)
    mean_x = 2.0 * (jnp.sum(total[...] * lane_f, axis=1, keepdims=True) / in_all) / (COLS - 1) - 1.0
    mean_y = 2.0 * (jnp.sum(total_row[...], axis=1, keepdims=True) / in_all) / (frame_rows - 1) - 1.0
    share = scale / in_all
    grad = grads[...]
    grad_x, grad_y = grad[:, 0:1], grad[:, 1:2]
    center = grad_x * mean_x + grad_y * mean_y
    key_x = 2.0 * lane_f / (COLS - 1) - 1.0
    base[...] = (grad_x * key_x - center) * share
    tilt[...] = jnp.broadcast_to(grad_y * share, (2 * count, LANES))
    total_row[0:count, :] = jnp.where(lane[0:count, :] == 0, mean_x[0:count, :], mean_y[0:count, :])
    both[...] = jnp.zeros_like(both)

    def slopes(visit, part, kept):
        z = z_hi if visit < visits // 2 else 1 - z_hi
        for j in range(span // LANES):
            at = slice(visit * span + j * LANES, visit * span + (j + 1) * LANES)
            index = (visit % (visits // 2)) * 4 + j // rows_per_block + 2 * z
            key_y = 2.0 * (index * rows_per_block + j % rows_per_block).astype(jnp.float32) / (frame_rows - 1) - 1.0
            for step in range(count // SUB):
                rows = slice(step * SUB, (step + 1) * SUB)
                q_rows = slice(part * count + step * SUB, part * count + (step + 1) * SUB)
                value = kept[rows, at].astype(jnp.float32) * (base[q_rows, :] + tilt[q_rows, :] * key_y)
                kept[rows, at] = value.astype(jnp.bfloat16)

    def collect(visit):
        at = slice(visit * span, (visit + 1) * span)
        both[...] += dot(prob[:, at], keys[at, :], ((1,), (0,)))
        if visit < visits // 2:
            partial = dot(feat_turned[:, 0:count], prob[:, at], ((1,), (0,)))
            partial = partial + dot(feat_turned[:, count : 2 * count], prob_far[:, at], ((1,), (0,)))
            payload[2 * visit, :, 0:count] = partial[:, 0:count].astype(jnp.bfloat16)
            payload[2 * visit + 1, :, 0:count] = partial[:, count:span].astype(jnp.bfloat16)

    slopes(0, 0, prob)
    slopes(0, 1, prob_far)
    for visit in range(visits):
        collect(visit)
        if visit + 1 < visits:
            slopes(visit + 1, 0, prob)
        if visit + 1 < visits // 2:
            slopes(visit + 1, 1, prob_far)
    low[...] = both[...].astype(jnp.bfloat16)
    turned_q[...] = turned(q_own[...])
    turned_g[...] = turned(low[:, chans : 2 * chans])
    back_one[...] = dot(low[:, 0:chans], w, ((1,), (1,))).astype(jnp.bfloat16)
    term = dot(turned_q[...], low[:, 0:chans], ((1,), (0,)))
    term = (term + dot(turned_g[...], feat_q[0:count, :], ((1,), (0,)))).astype(jnp.bfloat16)
    for block in range(blocks):
        payload[block, :, count : count + chans] = term

    flipped = total_row[0:count, :].T
    q_lane = lax.broadcasted_iota(jnp.int32, (1, count), 1)
    q_x = 2.0 * (q_lane % COLS).astype(jnp.float32) / (COLS - 1) - 1.0
    q_y = 2.0 * (q_lane // COLS + here * rows_per_block).astype(jnp.float32) / (frame_rows - 1) - 1.0
    flow[0:1, :] = flipped[0:1, :] - q_x
    flow[1:2, :] = flipped[1:2, :] - q_y


def owner_kernel(arrived, weight, back_two):
    count, chans = back_two.shape
    total = arrived[0, :, 0:count].astype(jnp.float32)
    for block in range(1, arrived.shape[0]):
        total = total + arrived[block, :, 0:count].astype(jnp.float32)
    grad_two = total.T.astype(jnp.bfloat16)
    back_two[...] = dot(grad_two, weight[...], ((1,), (1,))).astype(jnp.bfloat16)


def whole(*shape):
    return pl.BlockSpec(shape, lambda i: (0,) * len(shape))


def on_device(frame_one, frame_two, weight, flow_grad):
    _, count, chans = frame_one.shape
    devices = lax.axis_size("pix")
    blocks = devices // 2
    frame_rows = count * devices // COLS
    scale = chans ** (-0.5)
    near = [[i for i in range(devices) if (i // 2) % 2 == z] for z in range(2)]
    across = [(i, i ^ 2) for i in range(devices)]

    one, two, grad = frame_one[0], frame_two[0], flow_grad[0]
    rows = count + 3 * GRAD_ROWS
    pairs = lax.axis_size("pair")
    chunk = chans // pairs
    half = blocks * count
    params = pltpu.CompilerParams(vmem_limit_bytes=VMEM_LIMIT)
    with jax.named_scope("frame_two_across"):
        far_two = lax.ppermute(two, "pix", across)
    packed = pl.pallas_call(
        pack_kernel,
        out_shape=jax.ShapeDtypeStruct((rows, chans), jnp.bfloat16),
        scratch_shapes=[pltpu.VMEM((GRAD_ROWS, LANES), jnp.float32)],
        name="pack",
    )(one, grad)
    with jax.named_scope("near_gather"):
        near_keys = lax.all_gather(two, "pix", axis=0, axis_index_groups=near)
    with jax.named_scope("frame_one_across"):
        later, near_keys = lax.optimization_barrier((packed, near_keys))
        packed_far = lax.ppermute(later, "pix", across)
    with jax.named_scope("far_gather"):
        far_keys = lax.all_gather(far_two, "pix", axis=0, axis_index_groups=near)

    flow, back_one, payload = pl.pallas_call(
        functools.partial(match_kernel, frame_rows, scale),
        grid=(1,),
        in_specs=[
            whole(blocks, count, chans),
            whole(blocks, count, chans),
            whole(count, chans),
            whole(2, count),
            whole(rows, chans),
            whole(chans, chans),
        ],
        out_specs=[whole(2, count), whole(count, chans), whole(blocks, chans, count + chans)],
        out_shape=[
            jax.ShapeDtypeStruct((2, count), jnp.float32),
            jax.ShapeDtypeStruct((count, chans), jnp.bfloat16),
            jax.ShapeDtypeStruct((blocks, chans, count + chans), jnp.bfloat16),
        ],
        scratch_shapes=[
            pltpu.VMEM((2 * half, 2 * chans), jnp.bfloat16),
            pltpu.VMEM((count, 2 * half), jnp.float32),
            pltpu.VMEM((count, 2 * half), jnp.float32),
            pltpu.VMEM((count, 2 * half), jnp.bfloat16),
            pltpu.VMEM((count, half), jnp.bfloat16),
            pltpu.VMEM((2 * count, chans), jnp.bfloat16),
            pltpu.VMEM((chans, 2 * count), jnp.bfloat16),
            pltpu.VMEM((2 * count, LANES), jnp.float32),
            pltpu.VMEM((2 * count, LANES), jnp.float32),
            pltpu.VMEM((2 * count, LANES), jnp.float32),
            pltpu.VMEM((2 * count, LANES), jnp.float32),
            pltpu.VMEM((2 * count, LANES), jnp.float32),
            pltpu.VMEM((2 * count, LANES), jnp.float32),
            pltpu.VMEM((count, 2 * chans), jnp.float32),
            pltpu.VMEM((count, 2 * chans), jnp.bfloat16),
            pltpu.VMEM((chans, count), jnp.bfloat16),
            pltpu.VMEM((chans, count), jnp.bfloat16),
            pltpu.VMEM((LANES, 2 * count), jnp.float32),
        ],
        compiler_params=params,
        cost_estimate=pl.CostEstimate(flops=6 * 2 * count * 2 * half * chans, bytes_accessed=8 * 2**20, transcendentals=0),
        name="match",
    )(near_keys, far_keys, one, grad, packed_far, weight)

    with jax.named_scope("partial_sums"):
        arrived = lax.all_to_all(payload, "pix", 0, 0, axis_index_groups=near)
    with jax.named_scope("weight_terms"):
        term = jnp.sum(arrived[:, :, count:].astype(jnp.float32), axis=0).astype(jnp.bfloat16)
        sent = jnp.repeat(term.reshape(pairs, chunk, chans), 2, axis=0)
        planes = [
            [p * devices + z * 2 + r for p in range(pairs) for z in range(2)]
            for r in [y * 4 + c for y in range(devices // 4) for c in range(2)]
        ]
        terms = lax.all_to_all(sent, ("pair", "pix"), 0, 0, axis_index_groups=planes)
        weight_grad = jnp.sum(terms.astype(jnp.float32), axis=0)

    back_two = pl.pallas_call(
        owner_kernel,
        out_shape=jax.ShapeDtypeStruct((count, chans), jnp.bfloat16),
        cost_estimate=pl.CostEstimate(flops=2 * count * chans * chans, bytes_accessed=2**20, transcendentals=0),
        name="owner",
    )(arrived, weight)
    return (flow[None], back_one[None], back_two[None], weight_grad)


def solution(mesh):
    return jax.shard_map(
        on_device,
        mesh=mesh,
        in_specs=(P("pair", "pix", None), P("pair", "pix", None), P(), P("pair", None, "pix")),
        out_specs=(
            P("pair", None, "pix"),
            P("pair", "pix", None),
            P("pair", "pix", None),
            P("pair", None),
        ),
        check_vma=False,
    )
```

```python
import functools

import jax
import jax.numpy as jnp
from jax import lax
from jax.experimental import pallas as pl
from jax.experimental.pallas import tpu as pltpu
from jax.sharding import PartitionSpec as P

COLS = 128
LANES = 128
SUB = 32
FIRST = 4
SECOND = 4
THIRD = 6
GRAD_ROWS = 16
VMEM_LIMIT = 40 * 1024 * 1024
LOG2E = 1.4426950408889634


def dot(a, b, contract):
    return lax.dot_general(a, b, (contract, ((), ())), preferred_element_type=jnp.float32)


def many(low, high, each, step):
    def body(i, _):
        for k in range(each):
            step(low + i * each + k, 0)
        return 0

    lax.fori_loop(0, (high - low) // each, body, 0)


def turned(a):
    return a.astype(jnp.float32).T.astype(jnp.bfloat16)


def lane_iota(rows):
    return lax.broadcasted_iota(jnp.int32, (rows, LANES), 1)


def parted(value):
    high = value.astype(jnp.bfloat16)
    rest = value - high.astype(jnp.float32)
    middle = rest.astype(jnp.bfloat16)
    return high, middle, (rest - middle.astype(jnp.float32)).astype(jnp.bfloat16)


def joined(ref, start, rows):
    total = ref[start : start + rows, :].astype(jnp.float32)
    for part in (1, 2):
        total = total + ref[start + part * rows : start + (part + 1) * rows, :].astype(jnp.float32)
    return total


def pack_kernel(one, grad, out, spread):
    count = one.shape[0]
    wide = count // LANES
    out[0:count, :] = one[...]
    spread[...] = jnp.zeros_like(spread)
    for which in range(2):
        for j in range(wide):
            spread[which * wide + j : which * wide + j + 1, :] = grad[which : which + 1, j * LANES : (j + 1) * LANES]
    for part, value in enumerate(parted(spread[...])):
        start = count + part * GRAD_ROWS
        out[start : start + GRAD_ROWS, :] = value


def match_kernel(
    frame_rows, scale,
    near_keys, far_keys, q_own, g_own, packed_far, weight,
    flow, back_one, payload,
    keys, score_far, score_own, prob, prob_far, feat_q, feat_turned, grads, top, total, total_row, base, tilt, both, low, turned_q, turned_g, wide_grad,
):
    blocks, count, chans = near_keys.shape[0], q_own.shape[0], q_own.shape[1]
    span = 2 * count
    visits = blocks
    rows_per_block = count // COLS
    tiles = 2 * blocks * rows_per_block
    unit = scale * LOG2E
    here = lax.axis_index("pix")
    z_hi = (here // 2) % 2
    w = weight[...]

    def frame_row(block, row):
        z = z_hi if block < blocks else 1 - z_hi
        place = block % blocks
        index = (place // 2) * 4 + place % 2 + 2 * z
        return (index * rows_per_block + row).astype(jnp.float32)

    feat_q[0:count, :] = dot(q_own[...], w, ((1,), (0,))).astype(jnp.bfloat16)
    feat_q[count : 2 * count, :] = dot(packed_far[0:count, :], w, ((1,), (0,))).astype(jnp.bfloat16)
    feat_turned[...] = turned(feat_q[...])
    wide_grad[...] = jnp.zeros_like(wide_grad)
    wide_grad[0:2, 0:count] = g_own[...]
    far_grad = joined(packed_far, count, GRAD_ROWS)
    for which in range(2):
        for j in range(rows_per_block):
            wide_grad[which : which + 1, count + j * LANES : count + (j + 1) * LANES] = far_grad[
                which * rows_per_block + j : which * rows_per_block + j + 1, :
            ]
    grads[...] = wide_grad[...].T

    def scores(visit, queries, part, score):
        start = pl.multiple_of(visit * span, span)
        out = dot(queries, keys[pl.ds(start, span), 0:chans], ((1,), (1,)))
        score[:, pl.ds(start, span)] = out
        rows = slice(part * count, (part + 1) * count)
        best = top[rows, :]
        for j in range(span // LANES):
            best = jnp.maximum(best, out[:, j * LANES : (j + 1) * LANES])
        top[rows, :] = best

    def weigh(start, size, part, score, kept, keep):
        rows = pl.ds(start, size)
        q_rows = pl.ds(part * count + start, size)
        peak = top[q_rows, :]
        in_all = jnp.zeros((size, LANES), jnp.float32)
        in_row = jnp.zeros((size, LANES), jnp.float32)
        for j in range(tiles):
            p = jnp.exp2(score[rows, j * LANES : (j + 1) * LANES] * unit - peak)
            in_all = in_all + p
            in_row = in_row + p * frame_row(j // rows_per_block, j % rows_per_block)
            if j < keep:
                kept[rows, j * LANES : (j + 1) * LANES] = p.astype(jnp.bfloat16)
        total[q_rows, :] = in_all
        total_row[q_rows, :] = in_row

    def settle(part):
        rows = slice(part * count, (part + 1) * count)
        top[rows, :] = jnp.broadcast_to(jnp.max(top[rows, :], axis=1, keepdims=True) * unit, (count, LANES))

    top[...] = jnp.full_like(top, -jnp.inf)

    def first(visit, source, begin):
        for half in range(2):
            start = pl.multiple_of((begin + visit) * span + half * count, count)
            raw = source[2 * visit + half]
            keys[pl.ds(start, count), 0:chans] = dot(raw, w, ((1,), (0,))).astype(jnp.bfloat16)
            keys[pl.ds(start, count), chans : 2 * chans] = raw
        scores(begin + visit, feat_q[count : 2 * count, :], 1, score_far)

    many(0, visits // 2, FIRST, lambda visit, _: first(visit, near_keys, 0))
    many(0, visits // 2, FIRST, lambda visit, _: first(visit, far_keys, visits // 2))
    settle(1)

    def second(block, _):
        scores(block, feat_q[0:count, :], 0, score_own)
        size = count // visits
        weigh(pl.multiple_of(block * size, size), size, 1, score_far, prob_far, tiles // 2)
        return 0

    many(0, visits, SECOND, second)
    settle(0)

    def third(step, _):
        weigh(pl.multiple_of(step * SUB, SUB), SUB, 0, score_own, prob, tiles)
        return 0

    many(0, count // SUB, THIRD, third)

    lane = lane_iota(2 * count)
    lane_f = lane.astype(jnp.float32)
    in_all = jnp.sum(total[...], axis=1, keepdims=True)
    mean_x = 2.0 * (jnp.sum(total[...] * lane_f, axis=1, keepdims=True) / in_all) / (COLS - 1) - 1.0
    mean_y = 2.0 * (jnp.sum(total_row[...], axis=1, keepdims=True) / in_all) / (frame_rows - 1) - 1.0
    share = scale / in_all
    grad = grads[...]
    grad_x, grad_y = grad[:, 0:1], grad[:, 1:2]
    center = grad_x * mean_x + grad_y * mean_y
    key_x = 2.0 * lane_f / (COLS - 1) - 1.0
    base[...] = (grad_x * key_x - center) * share
    tilt[...] = jnp.broadcast_to(grad_y * share, (2 * count, LANES))
    total_row[0:count, :] = jnp.where(lane[0:count, :] == 0, mean_x[0:count, :], mean_y[0:count, :])
    both[...] = jnp.zeros_like(both)

    def slopes(visit, part, kept):
        z = z_hi if visit < visits // 2 else 1 - z_hi
        for j in range(span // LANES):
            at = slice(visit * span + j * LANES, visit * span + (j + 1) * LANES)
            index = (visit % (visits // 2)) * 4 + j // rows_per_block + 2 * z
            key_y = 2.0 * (index * rows_per_block + j % rows_per_block).astype(jnp.float32) / (frame_rows - 1) - 1.0
            for step in range(count // SUB):
                rows = slice(step * SUB, (step + 1) * SUB)
                q_rows = slice(part * count + step * SUB, part * count + (step + 1) * SUB)
                value = kept[rows, at].astype(jnp.float32) * (base[q_rows, :] + tilt[q_rows, :] * key_y)
                kept[rows, at] = value.astype(jnp.bfloat16)

    def collect(visit):
        at = slice(visit * span, (visit + 1) * span)
        both[...] += dot(prob[:, at], keys[at, :], ((1,), (0,)))
        if visit < visits // 2:
            partial = dot(feat_turned[:, 0:count], prob[:, at], ((1,), (0,)))
            partial = partial + dot(feat_turned[:, count : 2 * count], prob_far[:, at], ((1,), (0,)))
            payload[2 * visit, :, 0:count] = partial[:, 0:count].astype(jnp.bfloat16)
            payload[2 * visit + 1, :, 0:count] = partial[:, count:span].astype(jnp.bfloat16)

    slopes(0, 0, prob)
    slopes(0, 1, prob_far)
    for visit in range(visits):
        collect(visit)
        if visit + 1 < visits:
            slopes(visit + 1, 0, prob)
        if visit + 1 < visits // 2:
            slopes(visit + 1, 1, prob_far)
    low[...] = both[...].astype(jnp.bfloat16)
    turned_q[...] = turned(q_own[...])
    turned_g[...] = turned(low[:, chans : 2 * chans])
    back_one[...] = dot(low[:, 0:chans], w, ((1,), (1,))).astype(jnp.bfloat16)
    term = dot(turned_q[...], low[:, 0:chans], ((1,), (0,)))
    term = (term + dot(turned_g[...], feat_q[0:count, :], ((1,), (0,)))).astype(jnp.bfloat16)
    for block in range(blocks):
        payload[block, :, count : count + chans] = term

    flipped = total_row[0:count, :].T
    q_lane = lax.broadcasted_iota(jnp.int32, (1, count), 1)
    q_x = 2.0 * (q_lane % COLS).astype(jnp.float32) / (COLS - 1) - 1.0
    q_y = 2.0 * (q_lane // COLS + here * rows_per_block).astype(jnp.float32) / (frame_rows - 1) - 1.0
    flow[0:1, :] = flipped[0:1, :] - q_x
    flow[1:2, :] = flipped[1:2, :] - q_y


def owner_kernel(arrived, weight, back_two):
    count, chans = back_two.shape
    total = arrived[0, :, 0:count].astype(jnp.float32)
    for block in range(1, arrived.shape[0]):
        total = total + arrived[block, :, 0:count].astype(jnp.float32)
    grad_two = total.T.astype(jnp.bfloat16)
    back_two[...] = dot(grad_two, weight[...], ((1,), (1,))).astype(jnp.bfloat16)


def whole(*shape):
    return pl.BlockSpec(shape, lambda i: (0,) * len(shape))


def on_device(frame_one, frame_two, weight, flow_grad):
    _, count, chans = frame_one.shape
    devices = lax.axis_size("pix")
    blocks = devices // 2
    frame_rows = count * devices // COLS
    scale = chans ** (-0.5)
    near = [[i for i in range(devices) if (i // 2) % 2 == z] for z in range(2)]
    across = [(i, i ^ 2) for i in range(devices)]

    one, two, grad = frame_one[0], frame_two[0], flow_grad[0]
    rows = count + 3 * GRAD_ROWS
    pairs = lax.axis_size("pair")
    chunk = chans // pairs
    half = blocks * count
    params = pltpu.CompilerParams(vmem_limit_bytes=VMEM_LIMIT)
    with jax.named_scope("frame_two_across"):
        far_two = lax.ppermute(two, "pix", across)
    packed = pl.pallas_call(
        pack_kernel,
        out_shape=jax.ShapeDtypeStruct((rows, chans), jnp.bfloat16),
        scratch_shapes=[pltpu.VMEM((GRAD_ROWS, LANES), jnp.float32)],
        name="pack",
    )(one, grad)
    with jax.named_scope("near_gather"):
        near_keys = lax.all_gather(two, "pix", axis=0, axis_index_groups=near)
    with jax.named_scope("frame_one_across"):
        later, near_keys = lax.optimization_barrier((packed, near_keys))
        packed_far = lax.ppermute(later, "pix", across)
    with jax.named_scope("far_gather"):
        far_keys = lax.all_gather(far_two, "pix", axis=0, axis_index_groups=near)

    flow, back_one, payload = pl.pallas_call(
        functools.partial(match_kernel, frame_rows, scale),
        grid=(1,),
        in_specs=[
            whole(blocks, count, chans),
            whole(blocks, count, chans),
            whole(count, chans),
            whole(2, count),
            whole(rows, chans),
            whole(chans, chans),
        ],
        out_specs=[whole(2, count), whole(count, chans), whole(blocks, chans, count + chans)],
        out_shape=[
            jax.ShapeDtypeStruct((2, count), jnp.float32),
            jax.ShapeDtypeStruct((count, chans), jnp.bfloat16),
            jax.ShapeDtypeStruct((blocks, chans, count + chans), jnp.bfloat16),
        ],
        scratch_shapes=[
            pltpu.VMEM((2 * half, 2 * chans), jnp.bfloat16),
            pltpu.VMEM((count, 2 * half), jnp.float32),
            pltpu.VMEM((count, 2 * half), jnp.float32),
            pltpu.VMEM((count, 2 * half), jnp.bfloat16),
            pltpu.VMEM((count, half), jnp.bfloat16),
            pltpu.VMEM((2 * count, chans), jnp.bfloat16),
            pltpu.VMEM((chans, 2 * count), jnp.bfloat16),
            pltpu.VMEM((2 * count, LANES), jnp.float32),
            pltpu.VMEM((2 * count, LANES), jnp.float32),
            pltpu.VMEM((2 * count, LANES), jnp.float32),
            pltpu.VMEM((2 * count, LANES), jnp.float32),
            pltpu.VMEM((2 * count, LANES), jnp.float32),
            pltpu.VMEM((2 * count, LANES), jnp.float32),
            pltpu.VMEM((count, 2 * chans), jnp.float32),
            pltpu.VMEM((count, 2 * chans), jnp.bfloat16),
            pltpu.VMEM((chans, count), jnp.bfloat16),
            pltpu.VMEM((chans, count), jnp.bfloat16),
            pltpu.VMEM((LANES, 2 * count), jnp.float32),
        ],
        compiler_params=params,
        cost_estimate=pl.CostEstimate(flops=6 * 2 * count * 2 * half * chans, bytes_accessed=8 * 2**20, transcendentals=0),
        name="match",
    )(near_keys, far_keys, one, grad, packed_far, weight)

    with jax.named_scope("partial_sums"):
        arrived = lax.all_to_all(payload, "pix", 0, 0, axis_index_groups=near)
    with jax.named_scope("weight_terms"):
        term = jnp.sum(arrived[:, :, count:].astype(jnp.float32), axis=0).astype(jnp.bfloat16)
        sent = jnp.repeat(term.reshape(pairs, chunk, chans), 2, axis=0)
        planes = [
            [p * devices + z * 2 + r for p in range(pairs) for z in range(2)]
            for r in [y * 4 + c for y in range(devices // 4) for c in range(2)]
        ]
        terms = lax.all_to_all(sent, ("pair", "pix"), 0, 0, axis_index_groups=planes)
        weight_grad = jnp.sum(terms.astype(jnp.float32), axis=0)

    back_two = pl.pallas_call(
        owner_kernel,
        out_shape=jax.ShapeDtypeStruct((count, chans), jnp.bfloat16),
        cost_estimate=pl.CostEstimate(flops=2 * count * chans * chans, bytes_accessed=2**20, transcendentals=0),
        name="owner",
    )(arrived, weight)
    return (flow[None], back_one[None], back_two[None], weight_grad)


def solution(mesh):
    return jax.shard_map(
        on_device,
        mesh=mesh,
        in_specs=(P("pair", "pix", None), P("pair", "pix", None), P(), P("pair", None, "pix")),
        out_specs=(
            P("pair", None, "pix"),
            P("pair", "pix", None),
            P("pair", "pix", None),
            P("pair", None),
        ),
        check_vma=False,
    )
```

```python
import functools

import jax
import jax.numpy as jnp
from jax import lax
from jax.experimental import pallas as pl
from jax.experimental.pallas import tpu as pltpu
from jax.sharding import PartitionSpec as P

COLS = 128
LANES = 128
SUB = 32
FIRST = 4
SECOND_ROWS = 48
THIRD = 6
GRAD_ROWS = 16
VMEM_LIMIT = 40 * 1024 * 1024
LOG2E = 1.4426950408889634


def dot(a, b, contract):
    return lax.dot_general(a, b, (contract, ((), ())), preferred_element_type=jnp.float32)


def many(low, high, each, step):
    def body(i, _):
        for k in range(each):
            step(low + i * each + k, 0)
        return 0

    lax.fori_loop(0, (high - low) // each, body, 0)


def turned(a):
    return a.astype(jnp.float32).T.astype(jnp.bfloat16)


def lane_iota(rows):
    return lax.broadcasted_iota(jnp.int32, (rows, LANES), 1)


def parted(value):
    high = value.astype(jnp.bfloat16)
    rest = value - high.astype(jnp.float32)
    middle = rest.astype(jnp.bfloat16)
    return high, middle, (rest - middle.astype(jnp.float32)).astype(jnp.bfloat16)


def joined(ref, start, rows):
    total = ref[start : start + rows, :].astype(jnp.float32)
    for part in (1, 2):
        total = total + ref[start + part * rows : start + (part + 1) * rows, :].astype(jnp.float32)
    return total


def pack_kernel(one, two, grad, out, spread):
    count = one.shape[0]
    wide = count // LANES
    out[0:count, :] = two[...]
    out[count : 2 * count, :] = one[...]
    spread[...] = jnp.zeros_like(spread)
    for which in range(2):
        for j in range(wide):
            spread[which * wide + j : which * wide + j + 1, :] = grad[which : which + 1, j * LANES : (j + 1) * LANES]
    for part, value in enumerate(parted(spread[...])):
        start = 2 * count + part * GRAD_ROWS
        out[start : start + GRAD_ROWS, :] = value


def frame_row(z, block, row, rows_per_block):
    index = (block // 2) * 4 + block % 2 + 2 * z
    return (index * rows_per_block + row).astype(jnp.float32)


def take_scores(queries, keys, visit, span, top, out_rows, score, score_visit):
    start = pl.multiple_of(visit * span, span)
    chans = queries.shape[1]
    out = dot(queries, keys[pl.ds(start, span), 0:chans], ((1,), (1,)))
    score[:, pl.ds(pl.multiple_of(score_visit * span, span), span)] = out
    best = top[out_rows, :]
    for j in range(span // LANES):
        best = jnp.maximum(best, out[:, j * LANES : (j + 1) * LANES])
    top[out_rows, :] = best


def weigh_rows(score, rows, peak, zs, rows_per_block, unit, kept, keep):
    size = peak.shape[0]
    in_all = jnp.zeros((size, LANES), jnp.float32)
    in_row = jnp.zeros((size, LANES), jnp.float32)
    blocks = len(zs)
    for j in range(blocks * rows_per_block):
        block = j // rows_per_block
        p = jnp.exp2(score[rows, j * LANES : (j + 1) * LANES] * unit - peak)
        in_all = in_all + p
        in_row = in_row + p * frame_row(zs[block][0], zs[block][1], j % rows_per_block, rows_per_block)
        if j < keep:
            kept[rows, j * LANES : (j + 1) * LANES] = p.astype(jnp.bfloat16)
    return in_all, in_row


def near_kernel(scale, near_keys, q_own, weight, keys, prob, stat, score, feat, top):
    blocks, count, chans = near_keys.shape
    span, visits = 2 * count, blocks // 2
    rows_per_block = count // COLS
    tiles = blocks * rows_per_block
    unit = scale * LOG2E
    z_hi = (lax.axis_index("pix") // 2) % 2
    w = weight[...]
    feat[...] = dot(q_own[...], w, ((1,), (0,))).astype(jnp.bfloat16)
    top[...] = jnp.full_like(top, -jnp.inf)

    def step(visit, _):
        for half in range(2):
            start = pl.multiple_of(visit * span + half * count, count)
            raw = near_keys[2 * visit + half]
            keys[pl.ds(start, count), 0:chans] = dot(raw, w, ((1,), (0,))).astype(jnp.bfloat16)
            keys[pl.ds(start, count), chans : 2 * chans] = raw
        take_scores(feat[...], keys, visit, span, top, slice(0, count), score, visit)

    many(0, visits, FIRST, step)
    stat[0] = jnp.broadcast_to(jnp.max(top[...], axis=1, keepdims=True) * unit, (count, LANES))
    zs = [(z_hi, block) for block in range(blocks)]

    def weigh(step, _):
        rows = pl.ds(pl.multiple_of(step * SUB, SUB), SUB)
        stat[1, rows, :], stat[2, rows, :] = weigh_rows(score, rows, stat[0, rows, :], zs, rows_per_block, unit, prob, tiles)

    many(0, count // SUB, THIRD, weigh)


def match_kernel(
    frame_rows, scale,
    near_feat, near_prob, near_stat, far_keys, q_own, g_own, packed_far, weight,
    flow, back_one, payload,
    keys, score_far, score_own, prob, slope_near, prob_far, feat_q, feat_turned, grads, top, total, total_row, base, tilt, both, low, turned_q, turned_g, wide_grad,
):
    blocks, count, chans = far_keys.shape[0], q_own.shape[0], q_own.shape[1]
    span = 2 * count
    visits = blocks
    rows_per_block = count // COLS
    tiles = 2 * blocks * rows_per_block
    unit = scale * LOG2E
    here = lax.axis_index("pix")
    z_hi = (here // 2) % 2
    w = weight[...]

    feat_q[0:count, :] = dot(q_own[...], w, ((1,), (0,))).astype(jnp.bfloat16)
    feat_q[count : 2 * count, :] = dot(packed_far[count : 2 * count, :], w, ((1,), (0,))).astype(jnp.bfloat16)
    feat_turned[...] = turned(feat_q[...])
    wide_grad[...] = jnp.zeros_like(wide_grad)
    wide_grad[0:2, 0:count] = g_own[...]
    far_grad = joined(packed_far, 2 * count, GRAD_ROWS)
    for which in range(2):
        for j in range(rows_per_block):
            wide_grad[which : which + 1, count + j * LANES : count + (j + 1) * LANES] = far_grad[
                which * rows_per_block + j : which * rows_per_block + j + 1, :
            ]
    grads[...] = wide_grad[...].T

    half_visits = visits // 2
    half = blocks * count
    own, other = slice(0, count), slice(count, 2 * count)
    both_halves = [(z_hi, block) for block in range(blocks)] + [(1 - z_hi, block) for block in range(blocks)]

    def settle(rows):
        top[rows, :] = jnp.broadcast_to(jnp.max(top[rows, :], axis=1, keepdims=True) * unit, (count, LANES))

    top[...] = jnp.full_like(top, -jnp.inf)

    def near_visit(visit, _):
        take_scores(feat_q[other, :], near_feat, visit, span, top, other, score_far, visit)

    def far_visit(visit, _):
        for part in range(2):
            start = pl.multiple_of(visit * span + part * count, count)
            raw = far_keys[2 * visit + part]
            keys[pl.ds(start, count), 0:chans] = dot(raw, w, ((1,), (0,))).astype(jnp.bfloat16)
            keys[pl.ds(start, count), chans : 2 * chans] = raw
        take_scores(feat_q[other, :], keys, visit, span, top, other, score_far, half_visits + visit)

    many(0, half_visits, FIRST, near_visit)
    many(0, half_visits, FIRST, far_visit)
    settle(other)

    def second(visit, _):
        take_scores(feat_q[own, :], keys, visit, span, top, own, score_own, visit)
        size = SECOND_ROWS
        for part in range(count // size // half_visits):
            start = pl.multiple_of((visit * (count // size // half_visits) + part) * size, size)
            rows, q_rows = pl.ds(start, size), pl.ds(count + start, size)
            total[q_rows, :], total_row[q_rows, :] = weigh_rows(
                score_far, rows, top[q_rows, :], both_halves, rows_per_block, unit, prob_far, tiles // 2
            )

    many(0, half_visits, FIRST, second)
    settle(own)

    def third(step, _):
        rows = pl.ds(pl.multiple_of(step * SUB, SUB), SUB)
        total[rows, :], total_row[rows, :] = weigh_rows(
            score_own, rows, top[rows, :], both_halves[blocks:], rows_per_block, unit, prob, tiles // 2
        )

    many(0, count // SUB, THIRD, third)
    peak = jnp.maximum(top[own, :], near_stat[0])
    by_near, by_far = jnp.exp2(near_stat[0] - peak), jnp.exp2(top[own, :] - peak)
    total[own, :] = total[own, :] * by_far + near_stat[1] * by_near
    total_row[own, :] = total_row[own, :] * by_far + near_stat[2] * by_near

    lane = lane_iota(2 * count)
    lane_f = lane.astype(jnp.float32)
    in_all = jnp.sum(total[...], axis=1, keepdims=True)
    mean_x = 2.0 * (jnp.sum(total[...] * lane_f, axis=1, keepdims=True) / in_all) / (COLS - 1) - 1.0
    mean_y = 2.0 * (jnp.sum(total_row[...], axis=1, keepdims=True) / in_all) / (frame_rows - 1) - 1.0
    share = scale / in_all
    grad = grads[...]
    grad_x, grad_y = grad[:, 0:1], grad[:, 1:2]
    center = grad_x * mean_x + grad_y * mean_y
    key_x = 2.0 * lane_f / (COLS - 1) - 1.0
    whole_base = (grad_x * key_x - center) * share
    whole_tilt = jnp.broadcast_to(grad_y * share, (2 * count, LANES))
    base[0:count, :] = whole_base[0:count, :] * by_near
    tilt[0:count, :] = whole_tilt[0:count, :] * by_near
    base[count : 2 * count, :] = whole_base[count : 2 * count, :]
    tilt[count : 2 * count, :] = whole_tilt[count : 2 * count, :]
    base[2 * count : 3 * count, :] = whole_base[0:count, :] * by_far
    tilt[2 * count : 3 * count, :] = whole_tilt[0:count, :] * by_far
    total_row[0:count, :] = jnp.where(lane[0:count, :] == 0, mean_x[0:count, :], mean_y[0:count, :])
    both[...] = jnp.zeros_like(both)

    def slopes(visit, part, source, out):
        z = 1 - z_hi if part == 2 else z_hi
        for j in range(span // LANES):
            at = slice(visit * span + j * LANES, visit * span + (j + 1) * LANES)
            row = frame_row(z, 2 * visit + j // rows_per_block, j % rows_per_block, rows_per_block)
            key_y = 2.0 * row / (frame_rows - 1) - 1.0
            for step in range(count // SUB):
                rows = slice(step * SUB, (step + 1) * SUB)
                q_rows = slice(part * count + step * SUB, part * count + (step + 1) * SUB)
                value = source[rows, at].astype(jnp.float32) * (base[q_rows, :] + tilt[q_rows, :] * key_y)
                out[rows, at] = value.astype(jnp.bfloat16)

    def near_slopes(visit):
        slopes(visit, 0, near_prob, slope_near)
        slopes(visit, 1, prob_far, prob_far)

    def near_collect(visit):
        at = slice(visit * span, (visit + 1) * span)
        both[...] += dot(slope_near[:, at], near_feat[at, :], ((1,), (0,)))
        partial = dot(feat_turned[:, 0:count], slope_near[:, at], ((1,), (0,)))
        partial = partial + dot(feat_turned[:, count : 2 * count], prob_far[:, at], ((1,), (0,)))
        payload[2 * visit, :, 0:count] = partial[:, 0:count].astype(jnp.bfloat16)
        payload[2 * visit + 1, :, 0:count] = partial[:, count:span].astype(jnp.bfloat16)

    def far_collect(visit):
        at = slice(visit * span, (visit + 1) * span)
        both[...] += dot(prob[:, at], keys[at, :], ((1,), (0,)))

    near_slopes(0)
    for visit in range(half_visits):
        near_collect(visit)
        if visit + 1 < half_visits:
            near_slopes(visit + 1)
        else:
            slopes(0, 2, prob, prob)
    for visit in range(half_visits):
        far_collect(visit)
        if visit + 1 < half_visits:
            slopes(visit + 1, 2, prob, prob)
    low[...] = both[...].astype(jnp.bfloat16)
    turned_q[...] = turned(q_own[...])
    turned_g[...] = turned(low[:, chans : 2 * chans])
    back_one[...] = dot(low[:, 0:chans], w, ((1,), (1,))).astype(jnp.bfloat16)
    term = dot(turned_q[...], low[:, 0:chans], ((1,), (0,)))
    term = (term + dot(turned_g[...], feat_q[0:count, :], ((1,), (0,)))).astype(jnp.bfloat16)
    for block in range(blocks):
        payload[block, :, count : count + chans] = term

    flipped = total_row[0:count, :].T
    q_lane = lax.broadcasted_iota(jnp.int32, (1, count), 1)
    q_x = 2.0 * (q_lane % COLS).astype(jnp.float32) / (COLS - 1) - 1.0
    q_y = 2.0 * (q_lane // COLS + here * rows_per_block).astype(jnp.float32) / (frame_rows - 1) - 1.0
    flow[0:1, :] = flipped[0:1, :] - q_x
    flow[1:2, :] = flipped[1:2, :] - q_y


def owner_kernel(arrived, weight, back_two):
    count, chans = back_two.shape
    total = arrived[0, :, 0:count].astype(jnp.float32)
    for block in range(1, arrived.shape[0]):
        total = total + arrived[block, :, 0:count].astype(jnp.float32)
    grad_two = total.T.astype(jnp.bfloat16)
    back_two[...] = dot(grad_two, weight[...], ((1,), (1,))).astype(jnp.bfloat16)


def whole(*shape):
    return pl.BlockSpec(shape, lambda i: (0,) * len(shape))


def on_device(frame_one, frame_two, weight, flow_grad):
    _, count, chans = frame_one.shape
    devices = lax.axis_size("pix")
    blocks = devices // 2
    frame_rows = count * devices // COLS
    scale = chans ** (-0.5)
    near = [[i for i in range(devices) if (i // 2) % 2 == z] for z in range(2)]
    across = [(i, i ^ 2) for i in range(devices)]

    one, two, grad = frame_one[0], frame_two[0], flow_grad[0]
    rows = 2 * count + 3 * GRAD_ROWS
    pairs = lax.axis_size("pair")
    chunk = chans // pairs
    half = blocks * count
    params = pltpu.CompilerParams(vmem_limit_bytes=VMEM_LIMIT)
    packed = pl.pallas_call(
        pack_kernel,
        out_shape=jax.ShapeDtypeStruct((rows, chans), jnp.bfloat16),
        scratch_shapes=[pltpu.VMEM((GRAD_ROWS, LANES), jnp.float32)],
        name="pack",
    )(one, two, grad)
    with jax.named_scope("frames_across"):
        packed_far = lax.ppermute(packed, "pix", across)
    with jax.named_scope("near_gather"):
        near_keys = lax.all_gather(two, "pix", axis=0, axis_index_groups=near)
    near_feat, near_prob, near_stat = pl.pallas_call(
        functools.partial(near_kernel, scale),
        grid=(1,),
        in_specs=[whole(blocks, count, chans), whole(count, chans), whole(chans, chans)],
        out_specs=[whole(half, 2 * chans), whole(count, half), whole(3, count, LANES)],
        out_shape=[
            jax.ShapeDtypeStruct((half, 2 * chans), jnp.bfloat16),
            jax.ShapeDtypeStruct((count, half), jnp.bfloat16),
            jax.ShapeDtypeStruct((3, count, LANES), jnp.float32),
        ],
        scratch_shapes=[
            pltpu.VMEM((count, half), jnp.float32),
            pltpu.VMEM((count, chans), jnp.bfloat16),
            pltpu.VMEM((count, LANES), jnp.float32),
        ],
        compiler_params=params,
        cost_estimate=pl.CostEstimate(flops=2 * count * half * chans, bytes_accessed=6 * 2**20, transcendentals=0),
        name="near",
    )(near_keys, one, weight)
    with jax.named_scope("far_gather"):
        far_keys = lax.all_gather(packed_far[0:count], "pix", axis=0, axis_index_groups=near)

    flow, back_one, payload = pl.pallas_call(
        functools.partial(match_kernel, frame_rows, scale),
        grid=(1,),
        in_specs=[
            whole(half, 2 * chans),
            whole(count, half),
            whole(3, count, LANES),
            whole(blocks, count, chans),
            whole(count, chans),
            whole(2, count),
            whole(rows, chans),
            whole(chans, chans),
        ],
        out_specs=[whole(2, count), whole(count, chans), whole(blocks, chans, count + chans)],
        out_shape=[
            jax.ShapeDtypeStruct((2, count), jnp.float32),
            jax.ShapeDtypeStruct((count, chans), jnp.bfloat16),
            jax.ShapeDtypeStruct((blocks, chans, count + chans), jnp.bfloat16),
        ],
        scratch_shapes=[
            pltpu.VMEM((half, 2 * chans), jnp.bfloat16),
            pltpu.VMEM((count, 2 * half), jnp.float32),
            pltpu.VMEM((count, half), jnp.float32),
            pltpu.VMEM((count, half), jnp.bfloat16),
            pltpu.VMEM((count, half), jnp.bfloat16),
            pltpu.VMEM((count, half), jnp.bfloat16),
            pltpu.VMEM((2 * count, chans), jnp.bfloat16),
            pltpu.VMEM((chans, 2 * count), jnp.bfloat16),
            pltpu.VMEM((2 * count, LANES), jnp.float32),
            pltpu.VMEM((2 * count, LANES), jnp.float32),
            pltpu.VMEM((2 * count, LANES), jnp.float32),
            pltpu.VMEM((2 * count, LANES), jnp.float32),
            pltpu.VMEM((3 * count, LANES), jnp.float32),
            pltpu.VMEM((3 * count, LANES), jnp.float32),
            pltpu.VMEM((count, 2 * chans), jnp.float32),
            pltpu.VMEM((count, 2 * chans), jnp.bfloat16),
            pltpu.VMEM((chans, count), jnp.bfloat16),
            pltpu.VMEM((chans, count), jnp.bfloat16),
            pltpu.VMEM((LANES, 2 * count), jnp.float32),
        ],
        compiler_params=params,
        cost_estimate=pl.CostEstimate(flops=6 * 2 * count * 2 * half * chans, bytes_accessed=8 * 2**20, transcendentals=0),
        name="match",
    )(near_feat, near_prob, near_stat, far_keys, one, grad, packed_far, weight)

    with jax.named_scope("partial_sums"):
        arrived = lax.all_to_all(payload, "pix", 0, 0, axis_index_groups=near)
    with jax.named_scope("weight_terms"):
        term = jnp.sum(arrived[:, :, count:].astype(jnp.float32), axis=0).astype(jnp.bfloat16)
        sent = jnp.repeat(term.reshape(pairs, chunk, chans), 2, axis=0)
        planes = [
            [p * devices + z * 2 + r for p in range(pairs) for z in range(2)]
            for r in [y * 4 + c for y in range(devices // 4) for c in range(2)]
        ]
        terms = lax.all_to_all(sent, ("pair", "pix"), 0, 0, axis_index_groups=planes)
        weight_grad = jnp.sum(terms.astype(jnp.float32), axis=0)

    back_two = pl.pallas_call(
        owner_kernel,
        out_shape=jax.ShapeDtypeStruct((count, chans), jnp.bfloat16),
        cost_estimate=pl.CostEstimate(flops=2 * count * chans * chans, bytes_accessed=2**20, transcendentals=0),
        name="owner",
    )(arrived, weight)
    return (flow[None], back_one[None], back_two[None], weight_grad)


def solution(mesh):
    return jax.shard_map(
        on_device,
        mesh=mesh,
        in_specs=(P("pair", "pix", None), P("pair", "pix", None), P(), P("pair", None, "pix")),
        out_specs=(
            P("pair", None, "pix"),
            P("pair", "pix", None),
            P("pair", "pix", None),
            P("pair", None),
        ),
        check_vma=False,
    )
```

```python
import functools

import jax
import jax.numpy as jnp
from jax import lax
from jax.experimental import pallas as pl
from jax.experimental.pallas import tpu as pltpu
from jax.sharding import PartitionSpec as P

COLS = 128
LANES = 128
SUB = 32
FIRST = 4
SECOND_ROWS = 48
THIRD = 6
GRAD_ROWS = 16
VMEM_LIMIT = 40 * 1024 * 1024
LOG2E = 1.4426950408889634


def dot(a, b, contract):
    return lax.dot_general(a, b, (contract, ((), ())), preferred_element_type=jnp.float32)


def many(low, high, each, step):
    def body(i, _):
        for k in range(each):
            step(low + i * each + k, 0)
        return 0

    lax.fori_loop(0, (high - low) // each, body, 0)


def turned(a):
    return a.astype(jnp.float32).T.astype(jnp.bfloat16)


def lane_iota(rows):
    return lax.broadcasted_iota(jnp.int32, (rows, LANES), 1)


def parted(value):
    high = value.astype(jnp.bfloat16)
    rest = value - high.astype(jnp.float32)
    middle = rest.astype(jnp.bfloat16)
    return high, middle, (rest - middle.astype(jnp.float32)).astype(jnp.bfloat16)


def joined(ref, start, rows):
    total = ref[start : start + rows, :].astype(jnp.float32)
    for part in (1, 2):
        total = total + ref[start + part * rows : start + (part + 1) * rows, :].astype(jnp.float32)
    return total


def pack_kernel(one, two, grad, out, spread):
    count = one.shape[0]
    wide = count // LANES
    out[0:count, :] = two[...]
    out[count : 2 * count, :] = one[...]
    spread[...] = jnp.zeros_like(spread)
    for which in range(2):
        for j in range(wide):
            spread[which * wide + j : which * wide + j + 1, :] = grad[which : which + 1, j * LANES : (j + 1) * LANES]
    for part, value in enumerate(parted(spread[...])):
        start = 2 * count + part * GRAD_ROWS
        out[start : start + GRAD_ROWS, :] = value


def frame_row(z, block, row, rows_per_block):
    index = (block // 2) * 4 + block % 2 + 2 * z
    return (index * rows_per_block + row).astype(jnp.float32)


def take_scores(queries, keys, visit, span, top, out_rows, score, score_visit):
    start = pl.multiple_of(visit * span, span)
    chans = queries.shape[1]
    out = dot(queries, keys[pl.ds(start, span), 0:chans], ((1,), (1,)))
    score[:, pl.ds(pl.multiple_of(score_visit * span, span), span)] = out
    best = top[out_rows, :]
    for j in range(span // LANES):
        best = jnp.maximum(best, out[:, j * LANES : (j + 1) * LANES])
    top[out_rows, :] = best


def weigh_rows(score, rows, peak, zs, rows_per_block, unit, kept, keep):
    size = peak.shape[0]
    in_all = jnp.zeros((size, LANES), jnp.float32)
    in_row = jnp.zeros((size, LANES), jnp.float32)
    blocks = len(zs)
    for j in range(blocks * rows_per_block):
        block = j // rows_per_block
        p = jnp.exp2(score[rows, j * LANES : (j + 1) * LANES] * unit - peak)
        in_all = in_all + p
        in_row = in_row + p * frame_row(zs[block][0], zs[block][1], j % rows_per_block, rows_per_block)
        if j < keep:
            kept[rows, j * LANES : (j + 1) * LANES] = p.astype(jnp.bfloat16)
    return in_all, in_row


def near_kernel(scale, near_keys, one, weight, keys, prob, stat, score, feat, top, q_own, w_own, sems):
    blocks, count, chans = near_keys.shape
    span, visits = 2 * count, blocks // 2
    rows_per_block = count // COLS
    tiles = blocks * rows_per_block
    unit = scale * LOG2E
    z_hi = (lax.axis_index("pix") // 2) % 2
    copies = [pltpu.make_async_copy(one, q_own, sems.at[0]), pltpu.make_async_copy(weight, w_own, sems.at[1])]
    for copy in copies:
        copy.start()
    top[...] = jnp.full_like(top, -jnp.inf)
    for copy in copies:
        copy.wait()
    w = w_own[...]
    feat[...] = dot(q_own[...], w, ((1,), (0,))).astype(jnp.bfloat16)

    def step(visit, _):
        for half in range(2):
            start = pl.multiple_of(visit * span + half * count, count)
            raw = near_keys[2 * visit + half]
            keys[pl.ds(start, count), 0:chans] = dot(raw, w, ((1,), (0,))).astype(jnp.bfloat16)
            keys[pl.ds(start, count), chans : 2 * chans] = raw
        take_scores(feat[...], keys, visit, span, top, slice(0, count), score, visit)

    many(0, visits, FIRST, step)
    stat[0] = jnp.broadcast_to(jnp.max(top[...], axis=1, keepdims=True) * unit, (count, LANES))
    zs = [(z_hi, block) for block in range(blocks)]

    def weigh(step, _):
        rows = pl.ds(pl.multiple_of(step * SUB, SUB), SUB)
        stat[1, rows, :], stat[2, rows, :] = weigh_rows(score, rows, stat[0, rows, :], zs, rows_per_block, unit, prob, tiles)

    many(0, count // SUB, THIRD, weigh)


def match_kernel(
    frame_rows, scale,
    near_feat, near_prob, near_stat, far_keys, q_own, g_own, packed_far, weight,
    flow, back_one, payload,
    keys, score_far, score_own, prob, slope_near, prob_far, feat_q, feat_turned, grads, top, total, total_row, base, tilt, both, low, turned_q, turned_g, wide_grad,
):
    blocks, count, chans = far_keys.shape[0], q_own.shape[0], q_own.shape[1]
    span = 2 * count
    visits = blocks
    rows_per_block = count // COLS
    tiles = 2 * blocks * rows_per_block
    unit = scale * LOG2E
    here = lax.axis_index("pix")
    z_hi = (here // 2) % 2
    w = weight[...]

    feat_q[0:count, :] = dot(q_own[...], w, ((1,), (0,))).astype(jnp.bfloat16)
    feat_q[count : 2 * count, :] = dot(packed_far[count : 2 * count, :], w, ((1,), (0,))).astype(jnp.bfloat16)
    feat_turned[...] = turned(feat_q[...])
    wide_grad[...] = jnp.zeros_like(wide_grad)
    wide_grad[0:2, 0:count] = g_own[...]
    far_grad = joined(packed_far, 2 * count, GRAD_ROWS)
    for which in range(2):
        for j in range(rows_per_block):
            wide_grad[which : which + 1, count + j * LANES : count + (j + 1) * LANES] = far_grad[
                which * rows_per_block + j : which * rows_per_block + j + 1, :
            ]
    grads[...] = wide_grad[...].T

    half_visits = visits // 2
    half = blocks * count
    own, other = slice(0, count), slice(count, 2 * count)
    both_halves = [(z_hi, block) for block in range(blocks)] + [(1 - z_hi, block) for block in range(blocks)]

    def settle(rows):
        top[rows, :] = jnp.broadcast_to(jnp.max(top[rows, :], axis=1, keepdims=True) * unit, (count, LANES))

    top[...] = jnp.full_like(top, -jnp.inf)

    def near_visit(visit, _):
        take_scores(feat_q[other, :], near_feat, visit, span, top, other, score_far, visit)

    def far_visit(visit, _):
        for part in range(2):
            start = pl.multiple_of(visit * span + part * count, count)
            raw = far_keys[2 * visit + part]
            keys[pl.ds(start, count), 0:chans] = dot(raw, w, ((1,), (0,))).astype(jnp.bfloat16)
            keys[pl.ds(start, count), chans : 2 * chans] = raw
        take_scores(feat_q[other, :], keys, visit, span, top, other, score_far, half_visits + visit)

    many(0, half_visits, FIRST, near_visit)
    many(0, half_visits, FIRST, far_visit)
    settle(other)

    def second(visit, _):
        take_scores(feat_q[own, :], keys, visit, span, top, own, score_own, visit)
        size = SECOND_ROWS
        for part in range(count // size // half_visits):
            start = pl.multiple_of((visit * (count // size // half_visits) + part) * size, size)
            rows, q_rows = pl.ds(start, size), pl.ds(count + start, size)
            total[q_rows, :], total_row[q_rows, :] = weigh_rows(
                score_far, rows, top[q_rows, :], both_halves, rows_per_block, unit, prob_far, tiles // 2
            )

    many(0, half_visits, FIRST, second)
    settle(own)

    def third(step, _):
        rows = pl.ds(pl.multiple_of(step * SUB, SUB), SUB)
        total[rows, :], total_row[rows, :] = weigh_rows(
            score_own, rows, top[rows, :], both_halves[blocks:], rows_per_block, unit, prob, tiles // 2
        )

    many(0, count // SUB, THIRD, third)
    peak = jnp.maximum(top[own, :], near_stat[0])
    by_near, by_far = jnp.exp2(near_stat[0] - peak), jnp.exp2(top[own, :] - peak)
    total[own, :] = total[own, :] * by_far + near_stat[1] * by_near
    total_row[own, :] = total_row[own, :] * by_far + near_stat[2] * by_near

    lane = lane_iota(2 * count)
    lane_f = lane.astype(jnp.float32)
    in_all = jnp.sum(total[...], axis=1, keepdims=True)
    mean_x = 2.0 * (jnp.sum(total[...] * lane_f, axis=1, keepdims=True) / in_all) / (COLS - 1) - 1.0
    mean_y = 2.0 * (jnp.sum(total_row[...], axis=1, keepdims=True) / in_all) / (frame_rows - 1) - 1.0
    share = scale / in_all
    grad = grads[...]
    grad_x, grad_y = grad[:, 0:1], grad[:, 1:2]
    center = grad_x * mean_x + grad_y * mean_y
    key_x = 2.0 * lane_f / (COLS - 1) - 1.0
    whole_base = (grad_x * key_x - center) * share
    whole_tilt = jnp.broadcast_to(grad_y * share, (2 * count, LANES))
    base[0:count, :] = whole_base[0:count, :] * by_near
    tilt[0:count, :] = whole_tilt[0:count, :] * by_near
    base[count : 2 * count, :] = whole_base[count : 2 * count, :]
    tilt[count : 2 * count, :] = whole_tilt[count : 2 * count, :]
    base[2 * count : 3 * count, :] = whole_base[0:count, :] * by_far
    tilt[2 * count : 3 * count, :] = whole_tilt[0:count, :] * by_far
    total_row[0:count, :] = jnp.where(lane[0:count, :] == 0, mean_x[0:count, :], mean_y[0:count, :])
    both[...] = jnp.zeros_like(both)

    def slopes(visit, part, source, out):
        z = 1 - z_hi if part == 2 else z_hi
        for j in range(span // LANES):
            at = slice(visit * span + j * LANES, visit * span + (j + 1) * LANES)
            row = frame_row(z, 2 * visit + j // rows_per_block, j % rows_per_block, rows_per_block)
            key_y = 2.0 * row / (frame_rows - 1) - 1.0
            for step in range(count // SUB):
                rows = slice(step * SUB, (step + 1) * SUB)
                q_rows = slice(part * count + step * SUB, part * count + (step + 1) * SUB)
                value = source[rows, at].astype(jnp.float32) * (base[q_rows, :] + tilt[q_rows, :] * key_y)
                out[rows, at] = value.astype(jnp.bfloat16)

    def near_slopes(visit):
        slopes(visit, 0, near_prob, slope_near)
        slopes(visit, 1, prob_far, prob_far)

    def near_collect(visit):
        at = slice(visit * span, (visit + 1) * span)
        both[...] += dot(slope_near[:, at], near_feat[at, :], ((1,), (0,)))
        partial = dot(feat_turned[:, 0:count], slope_near[:, at], ((1,), (0,)))
        partial = partial + dot(feat_turned[:, count : 2 * count], prob_far[:, at], ((1,), (0,)))
        payload[0, visit, :, 0:count] = partial[:, 0:count].astype(jnp.bfloat16)
        payload[1, visit, :, 0:count] = partial[:, count:span].astype(jnp.bfloat16)

    def far_collect(visit):
        at = slice(visit * span, (visit + 1) * span)
        both[...] += dot(prob[:, at], keys[at, :], ((1,), (0,)))

    near_slopes(0)
    for visit in range(half_visits):
        near_collect(visit)
        if visit + 1 < half_visits:
            near_slopes(visit + 1)
        else:
            slopes(0, 2, prob, prob)
    for visit in range(half_visits):
        far_collect(visit)
        if visit + 1 < half_visits:
            slopes(visit + 1, 2, prob, prob)
    low[...] = both[...].astype(jnp.bfloat16)
    turned_q[...] = turned(q_own[...])
    turned_g[...] = turned(low[:, chans : 2 * chans])
    back_one[...] = dot(low[:, 0:chans], w, ((1,), (1,))).astype(jnp.bfloat16)
    term = dot(turned_q[...], low[:, 0:chans], ((1,), (0,)))
    term = (term + dot(turned_g[...], feat_q[0:count, :], ((1,), (0,)))).astype(jnp.bfloat16)
    for core in range(2):
        for place in range(blocks // 2):
            payload[core, place, :, count : count + chans] = term

    flipped = total_row[0:count, :].T
    q_lane = lax.broadcasted_iota(jnp.int32, (1, count), 1)
    q_x = 2.0 * (q_lane % COLS).astype(jnp.float32) / (COLS - 1) - 1.0
    q_y = 2.0 * (q_lane // COLS + here * rows_per_block).astype(jnp.float32) / (frame_rows - 1) - 1.0
    flow[0:1, :] = flipped[0:1, :] - q_x
    flow[1:2, :] = flipped[1:2, :] - q_y


def owner_kernel(arrived, weight, back_two):
    count, chans = back_two.shape
    total = arrived[0, :, 0:count].astype(jnp.float32)
    for block in range(1, arrived.shape[0]):
        total = total + arrived[block, :, 0:count].astype(jnp.float32)
    grad_two = total.T.astype(jnp.bfloat16)
    back_two[...] = dot(grad_two, weight[...], ((1,), (1,))).astype(jnp.bfloat16)


def whole(*shape):
    return pl.BlockSpec(shape, lambda i: (0,) * len(shape))


def on_device(frame_one, frame_two, weight, flow_grad):
    _, count, chans = frame_one.shape
    devices = lax.axis_size("pix")
    blocks = devices // 2
    frame_rows = count * devices // COLS
    scale = chans ** (-0.5)
    near = [[i for i in range(devices) if (i // 2) % 2 == z] for z in range(2)]
    across = [(i, i ^ 2) for i in range(devices)]

    one, two, grad = frame_one[0], frame_two[0], flow_grad[0]
    rows = 2 * count + 3 * GRAD_ROWS
    pairs = lax.axis_size("pair")
    chunk = chans // pairs
    half = blocks * count
    params = pltpu.CompilerParams(vmem_limit_bytes=VMEM_LIMIT)
    packed = pl.pallas_call(
        pack_kernel,
        out_shape=jax.ShapeDtypeStruct((rows, chans), jnp.bfloat16),
        scratch_shapes=[pltpu.VMEM((GRAD_ROWS, LANES), jnp.float32)],
        name="pack",
    )(one, two, grad)
    with jax.named_scope("frames_across"):
        packed_far = lax.ppermute(packed, "pix", across)
    with jax.named_scope("near_gather"):
        near_keys = lax.all_gather(two, "pix", axis=0, axis_index_groups=near)
    near_feat, near_prob, near_stat = pl.pallas_call(
        functools.partial(near_kernel, scale),
        grid=(1,),
        in_specs=[whole(blocks, count, chans), pl.BlockSpec(memory_space=pltpu.HBM), pl.BlockSpec(memory_space=pltpu.HBM)],
        out_specs=[whole(half, 2 * chans), whole(count, half), whole(3, count, LANES)],
        out_shape=[
            jax.ShapeDtypeStruct((half, 2 * chans), jnp.bfloat16),
            jax.ShapeDtypeStruct((count, half), jnp.bfloat16),
            jax.ShapeDtypeStruct((3, count, LANES), jnp.float32),
        ],
        scratch_shapes=[
            pltpu.VMEM((count, half), jnp.float32),
            pltpu.VMEM((count, chans), jnp.bfloat16),
            pltpu.VMEM((count, LANES), jnp.float32),
            pltpu.VMEM((count, chans), jnp.bfloat16),
            pltpu.VMEM((chans, chans), jnp.bfloat16),
            pltpu.SemaphoreType.DMA((2,)),
        ],
        compiler_params=params,
        cost_estimate=pl.CostEstimate(flops=2 * count * half * chans, bytes_accessed=6 * 2**20, transcendentals=0),
        name="near",
    )(near_keys, one, weight)
    with jax.named_scope("far_gather"):
        far_keys = lax.all_gather(packed_far[0:count], "pix", axis=0, axis_index_groups=near)

    flow, back_one, payload = pl.pallas_call(
        functools.partial(match_kernel, frame_rows, scale),
        grid=(1,),
        in_specs=[
            whole(half, 2 * chans),
            whole(count, half),
            whole(3, count, LANES),
            whole(blocks, count, chans),
            whole(count, chans),
            whole(2, count),
            whole(rows, chans),
            whole(chans, chans),
        ],
        out_specs=[whole(2, count), whole(count, chans), whole(2, blocks // 2, chans, count + chans)],
        out_shape=[
            jax.ShapeDtypeStruct((2, count), jnp.float32),
            jax.ShapeDtypeStruct((count, chans), jnp.bfloat16),
            jax.ShapeDtypeStruct((2, blocks // 2, chans, count + chans), jnp.bfloat16),
        ],
        scratch_shapes=[
            pltpu.VMEM((half, 2 * chans), jnp.bfloat16),
            pltpu.VMEM((count, 2 * half), jnp.float32),
            pltpu.VMEM((count, half), jnp.float32),
            pltpu.VMEM((count, half), jnp.bfloat16),
            pltpu.VMEM((count, half), jnp.bfloat16),
            pltpu.VMEM((count, half), jnp.bfloat16),
            pltpu.VMEM((2 * count, chans), jnp.bfloat16),
            pltpu.VMEM((chans, 2 * count), jnp.bfloat16),
            pltpu.VMEM((2 * count, LANES), jnp.float32),
            pltpu.VMEM((2 * count, LANES), jnp.float32),
            pltpu.VMEM((2 * count, LANES), jnp.float32),
            pltpu.VMEM((2 * count, LANES), jnp.float32),
            pltpu.VMEM((3 * count, LANES), jnp.float32),
            pltpu.VMEM((3 * count, LANES), jnp.float32),
            pltpu.VMEM((count, 2 * chans), jnp.float32),
            pltpu.VMEM((count, 2 * chans), jnp.bfloat16),
            pltpu.VMEM((chans, count), jnp.bfloat16),
            pltpu.VMEM((chans, count), jnp.bfloat16),
            pltpu.VMEM((LANES, 2 * count), jnp.float32),
        ],
        compiler_params=params,
        cost_estimate=pl.CostEstimate(flops=6 * 2 * count * 2 * half * chans, bytes_accessed=8 * 2**20, transcendentals=0),
        name="match",
    )(near_feat, near_prob, near_stat, far_keys, one, grad, packed_far, weight)

    with jax.named_scope("partial_sums"):
        cores = [[2 * i, 2 * i + 1] for i in range(blocks)]
        chips = [[y * 4 + r for y in range(devices // 4)] for r in range(4)]
        swapped = lax.all_to_all(payload, "pix", 0, 0, axis_index_groups=cores)
        summed = (swapped[0].astype(jnp.float32) + swapped[1].astype(jnp.float32)).astype(jnp.bfloat16)
        arrived = lax.all_to_all(summed, "pix", 0, 0, axis_index_groups=chips)
    with jax.named_scope("weight_terms"):
        term = jnp.sum(arrived[:, :, count:].astype(jnp.float32), axis=0).astype(jnp.bfloat16)
        sent = jnp.repeat(term.reshape(pairs, chunk, chans), 2, axis=0)
        planes = [
            [p * devices + z * 2 + r for p in range(pairs) for z in range(2)]
            for r in [y * 4 + c for y in range(devices // 4) for c in range(2)]
        ]
        terms = lax.all_to_all(sent, ("pair", "pix"), 0, 0, axis_index_groups=planes)
        weight_grad = jnp.sum(terms.astype(jnp.float32), axis=0)

    back_two = pl.pallas_call(
        owner_kernel,
        out_shape=jax.ShapeDtypeStruct((count, chans), jnp.bfloat16),
        cost_estimate=pl.CostEstimate(flops=2 * count * chans * chans, bytes_accessed=2**20, transcendentals=0),
        name="owner",
    )(arrived, weight)
    return (flow[None], back_one[None], back_two[None], weight_grad)


def solution(mesh):
    return jax.shard_map(
        on_device,
        mesh=mesh,
        in_specs=(P("pair", "pix", None), P("pair", "pix", None), P(), P("pair", None, "pix")),
        out_specs=(
            P("pair", None, "pix"),
            P("pair", "pix", None),
            P("pair", "pix", None),
            P("pair", None),
        ),
        check_vma=False,
    )
```

```python
import functools

import jax
import jax.numpy as jnp
from jax import lax
from jax.experimental import pallas as pl
from jax.experimental.pallas import tpu as pltpu
from jax.sharding import PartitionSpec as P

COLS = 128
LANES = 128
SUB = 32
FIRST = 4
SECOND_ROWS = 48
THIRD = 6
GRAD_ROWS = 16
VMEM_LIMIT = 40 * 1024 * 1024
LOG2E = 1.4426950408889634


def dot(a, b, contract):
    return lax.dot_general(a, b, (contract, ((), ())), preferred_element_type=jnp.float32)


def many(low, high, each, step):
    def body(i, _):
        for k in range(each):
            step(low + i * each + k, 0)
        return 0

    lax.fori_loop(0, (high - low) // each, body, 0)


def turned(a):
    return a.astype(jnp.float32).T.astype(jnp.bfloat16)


def lane_iota(rows):
    return lax.broadcasted_iota(jnp.int32, (rows, LANES), 1)


def parted(value):
    high = value.astype(jnp.bfloat16)
    rest = value - high.astype(jnp.float32)
    middle = rest.astype(jnp.bfloat16)
    return high, middle, (rest - middle.astype(jnp.float32)).astype(jnp.bfloat16)


def joined(ref, start, rows):
    total = ref[start : start + rows, :].astype(jnp.float32)
    for part in (1, 2):
        total = total + ref[start + part * rows : start + (part + 1) * rows, :].astype(jnp.float32)
    return total


def pack_kernel(one, two, grad, weight, out, small, spread):
    small[0 : one.shape[0], :] = one[...]
    small[one.shape[0] :, :] = weight[...]
    count = one.shape[0]
    wide = count // LANES
    out[0:count, :] = two[...]
    out[count : 2 * count, :] = one[...]
    spread[...] = jnp.zeros_like(spread)
    for which in range(2):
        for j in range(wide):
            spread[which * wide + j : which * wide + j + 1, :] = grad[which : which + 1, j * LANES : (j + 1) * LANES]
    for part, value in enumerate(parted(spread[...])):
        start = 2 * count + part * GRAD_ROWS
        out[start : start + GRAD_ROWS, :] = value


def frame_row(z, block, row, rows_per_block):
    index = (block // 2) * 4 + block % 2 + 2 * z
    return (index * rows_per_block + row).astype(jnp.float32)


def take_scores(queries, keys, visit, span, top, out_rows, score, score_visit):
    start = pl.multiple_of(visit * span, span)
    chans = queries.shape[1]
    out = dot(queries, keys[pl.ds(start, span), 0:chans], ((1,), (1,)))
    score[:, pl.ds(pl.multiple_of(score_visit * span, span), span)] = out
    best = top[out_rows, :]
    for j in range(span // LANES):
        best = jnp.maximum(best, out[:, j * LANES : (j + 1) * LANES])
    top[out_rows, :] = best


def weigh_rows(score, rows, peak, zs, rows_per_block, unit, kept, keep):
    size = peak.shape[0]
    in_all = jnp.zeros((size, LANES), jnp.float32)
    in_row = jnp.zeros((size, LANES), jnp.float32)
    blocks = len(zs)
    for j in range(blocks * rows_per_block):
        block = j // rows_per_block
        p = jnp.exp2(score[rows, j * LANES : (j + 1) * LANES] * unit - peak)
        in_all = in_all + p
        in_row = in_row + p * frame_row(zs[block][0], zs[block][1], j % rows_per_block, rows_per_block)
        if j < keep:
            kept[rows, j * LANES : (j + 1) * LANES] = p.astype(jnp.bfloat16)
    return in_all, in_row


def near_kernel(scale, near_keys, small, keys, prob, stat, flipped, score, feat, top):
    blocks, count, chans = near_keys.shape
    span, visits = 2 * count, blocks // 2
    rows_per_block = count // COLS
    tiles = blocks * rows_per_block
    unit = scale * LOG2E
    z_hi = (lax.axis_index("pix") // 2) % 2
    w = small[count : count + chans, :]
    feat[...] = dot(small[0:count, :], w, ((1,), (0,))).astype(jnp.bfloat16)
    flipped[0] = turned(feat[...])
    flipped[1] = turned(small[0:count, :])
    top[...] = jnp.full_like(top, -jnp.inf)

    def step(visit, _):
        for half in range(2):
            start = pl.multiple_of(visit * span + half * count, count)
            raw = near_keys[2 * visit + half]
            keys[pl.ds(start, count), 0:chans] = dot(raw, w, ((1,), (0,))).astype(jnp.bfloat16)
            keys[pl.ds(start, count), chans : 2 * chans] = raw
        take_scores(feat[...], keys, visit, span, top, slice(0, count), score, visit)

    many(0, visits, FIRST, step)
    stat[0] = jnp.broadcast_to(jnp.max(top[...], axis=1, keepdims=True) * unit, (count, LANES))
    zs = [(z_hi, block) for block in range(blocks)]

    def weigh(step, _):
        rows = pl.ds(pl.multiple_of(step * SUB, SUB), SUB)
        stat[1, rows, :], stat[2, rows, :] = weigh_rows(score, rows, stat[0, rows, :], zs, rows_per_block, unit, prob, tiles)

    many(0, count // SUB, THIRD, weigh)


def match_kernel(
    frame_rows, scale,
    near_feat, near_prob, near_stat, near_turned, far_keys, q_own, g_own, packed_far, weight,
    flow, back_one, payload,
    keys, score_far, score_own, prob, slope_near, prob_far, feat_q, far_turned, grads, top, total, total_row, base, tilt, both, low, turned_g, wide_grad,
):
    blocks, count, chans = far_keys.shape[0], q_own.shape[0], q_own.shape[1]
    span = 2 * count
    visits = blocks
    rows_per_block = count // COLS
    tiles = 2 * blocks * rows_per_block
    unit = scale * LOG2E
    here = lax.axis_index("pix")
    z_hi = (here // 2) % 2
    w = weight[...]

    feat_q[0:count, :] = dot(q_own[...], w, ((1,), (0,))).astype(jnp.bfloat16)
    feat_q[count : 2 * count, :] = dot(packed_far[count : 2 * count, :], w, ((1,), (0,))).astype(jnp.bfloat16)
    far_turned[...] = turned(feat_q[count : 2 * count, :])
    wide_grad[...] = jnp.zeros_like(wide_grad)
    wide_grad[0:2, 0:count] = g_own[...]
    far_grad = joined(packed_far, 2 * count, GRAD_ROWS)
    for which in range(2):
        for j in range(rows_per_block):
            wide_grad[which : which + 1, count + j * LANES : count + (j + 1) * LANES] = far_grad[
                which * rows_per_block + j : which * rows_per_block + j + 1, :
            ]
    grads[...] = wide_grad[...].T

    half_visits = visits // 2
    half = blocks * count
    own, other = slice(0, count), slice(count, 2 * count)
    both_halves = [(z_hi, block) for block in range(blocks)] + [(1 - z_hi, block) for block in range(blocks)]

    def settle(rows):
        top[rows, :] = jnp.broadcast_to(jnp.max(top[rows, :], axis=1, keepdims=True) * unit, (count, LANES))

    top[...] = jnp.full_like(top, -jnp.inf)

    def near_visit(visit, _):
        take_scores(feat_q[other, :], near_feat, visit, span, top, other, score_far, visit)

    def far_visit(visit, _):
        for part in range(2):
            start = pl.multiple_of(visit * span + part * count, count)
            raw = far_keys[2 * visit + part]
            keys[pl.ds(start, count), 0:chans] = dot(raw, w, ((1,), (0,))).astype(jnp.bfloat16)
            keys[pl.ds(start, count), chans : 2 * chans] = raw
        take_scores(feat_q[other, :], keys, visit, span, top, other, score_far, half_visits + visit)

    many(0, half_visits, FIRST, near_visit)
    many(0, half_visits, FIRST, far_visit)
    settle(other)

    def second(visit, _):
        take_scores(feat_q[own, :], keys, visit, span, top, own, score_own, visit)
        size = SECOND_ROWS
        for part in range(count // size // half_visits):
            start = pl.multiple_of((visit * (count // size // half_visits) + part) * size, size)
            rows, q_rows = pl.ds(start, size), pl.ds(count + start, size)
            total[q_rows, :], total_row[q_rows, :] = weigh_rows(
                score_far, rows, top[q_rows, :], both_halves, rows_per_block, unit, prob_far, tiles // 2
            )

    many(0, half_visits, FIRST, second)
    settle(own)

    def third(step, _):
        rows = pl.ds(pl.multiple_of(step * SUB, SUB), SUB)
        total[rows, :], total_row[rows, :] = weigh_rows(
            score_own, rows, top[rows, :], both_halves[blocks:], rows_per_block, unit, prob, tiles // 2
        )

    many(0, count // SUB, THIRD, third)
    peak = jnp.maximum(top[own, :], near_stat[0])
    by_near, by_far = jnp.exp2(near_stat[0] - peak), jnp.exp2(top[own, :] - peak)
    total[own, :] = total[own, :] * by_far + near_stat[1] * by_near
    total_row[own, :] = total_row[own, :] * by_far + near_stat[2] * by_near

    lane = lane_iota(2 * count)
    lane_f = lane.astype(jnp.float32)
    in_all = jnp.sum(total[...], axis=1, keepdims=True)
    mean_x = 2.0 * (jnp.sum(total[...] * lane_f, axis=1, keepdims=True) / in_all) / (COLS - 1) - 1.0
    mean_y = 2.0 * (jnp.sum(total_row[...], axis=1, keepdims=True) / in_all) / (frame_rows - 1) - 1.0
    share = scale / in_all
    grad = grads[...]
    grad_x, grad_y = grad[:, 0:1], grad[:, 1:2]
    center = grad_x * mean_x + grad_y * mean_y
    key_x = 2.0 * lane_f / (COLS - 1) - 1.0
    whole_base = (grad_x * key_x - center) * share
    whole_tilt = jnp.broadcast_to(grad_y * share, (2 * count, LANES))
    base[0:count, :] = whole_base[0:count, :] * by_near
    tilt[0:count, :] = whole_tilt[0:count, :] * by_near
    base[count : 2 * count, :] = whole_base[count : 2 * count, :]
    tilt[count : 2 * count, :] = whole_tilt[count : 2 * count, :]
    base[2 * count : 3 * count, :] = whole_base[0:count, :] * by_far
    tilt[2 * count : 3 * count, :] = whole_tilt[0:count, :] * by_far
    total_row[0:count, :] = jnp.where(lane[0:count, :] == 0, mean_x[0:count, :], mean_y[0:count, :])
    both[...] = jnp.zeros_like(both)

    def slopes(visit, part, source, out):
        z = 1 - z_hi if part == 2 else z_hi
        for j in range(span // LANES):
            at = slice(visit * span + j * LANES, visit * span + (j + 1) * LANES)
            row = frame_row(z, 2 * visit + j // rows_per_block, j % rows_per_block, rows_per_block)
            key_y = 2.0 * row / (frame_rows - 1) - 1.0
            for step in range(count // SUB):
                rows = slice(step * SUB, (step + 1) * SUB)
                q_rows = slice(part * count + step * SUB, part * count + (step + 1) * SUB)
                value = source[rows, at].astype(jnp.float32) * (base[q_rows, :] + tilt[q_rows, :] * key_y)
                out[rows, at] = value.astype(jnp.bfloat16)

    def near_slopes(visit):
        slopes(visit, 0, near_prob, slope_near)
        slopes(visit, 1, prob_far, prob_far)

    def near_collect(visit):
        at = slice(visit * span, (visit + 1) * span)
        both[...] += dot(slope_near[:, at], near_feat[at, :], ((1,), (0,)))
        partial = dot(near_turned[0], slope_near[:, at], ((1,), (0,)))
        partial = partial + dot(far_turned[...], prob_far[:, at], ((1,), (0,)))
        payload[0, visit, :, 0:count] = partial[:, 0:count].astype(jnp.bfloat16)
        payload[1, visit, :, 0:count] = partial[:, count:span].astype(jnp.bfloat16)

    def far_collect(visit):
        at = slice(visit * span, (visit + 1) * span)
        both[...] += dot(prob[:, at], keys[at, :], ((1,), (0,)))

    near_slopes(0)
    for visit in range(half_visits):
        near_collect(visit)
        if visit + 1 < half_visits:
            near_slopes(visit + 1)
        else:
            slopes(0, 2, prob, prob)
    for visit in range(half_visits):
        far_collect(visit)
        if visit + 1 < half_visits:
            slopes(visit + 1, 2, prob, prob)
    low[...] = both[...].astype(jnp.bfloat16)
    turned_g[...] = turned(low[:, chans : 2 * chans])
    back_one[...] = dot(low[:, 0:chans], w, ((1,), (1,))).astype(jnp.bfloat16)
    term = dot(near_turned[1], low[:, 0:chans], ((1,), (0,)))
    term = (term + dot(turned_g[...], feat_q[0:count, :], ((1,), (0,)))).astype(jnp.bfloat16)
    for core in range(2):
        for place in range(blocks // 2):
            payload[core, place, :, count : count + chans] = term

    flipped = total_row[0:count, :].T
    q_lane = lax.broadcasted_iota(jnp.int32, (1, count), 1)
    q_x = 2.0 * (q_lane % COLS).astype(jnp.float32) / (COLS - 1) - 1.0
    q_y = 2.0 * (q_lane // COLS + here * rows_per_block).astype(jnp.float32) / (frame_rows - 1) - 1.0
    flow[0:1, :] = flipped[0:1, :] - q_x
    flow[1:2, :] = flipped[1:2, :] - q_y


def owner_kernel(arrived, weight, back_two):
    count, chans = back_two.shape
    total = arrived[0, :, 0:count].astype(jnp.float32)
    for block in range(1, arrived.shape[0]):
        total = total + arrived[block, :, 0:count].astype(jnp.float32)
    grad_two = total.T.astype(jnp.bfloat16)
    back_two[...] = dot(grad_two, weight[...], ((1,), (1,))).astype(jnp.bfloat16)


def whole(*shape):
    return pl.BlockSpec(shape, lambda i: (0,) * len(shape))


def on_device(frame_one, frame_two, weight, flow_grad):
    _, count, chans = frame_one.shape
    devices = lax.axis_size("pix")
    blocks = devices // 2
    frame_rows = count * devices // COLS
    scale = chans ** (-0.5)
    near = [[i for i in range(devices) if (i // 2) % 2 == z] for z in range(2)]
    across = [(i, i ^ 2) for i in range(devices)]

    one, two, grad = frame_one[0], frame_two[0], flow_grad[0]
    rows = 2 * count + 3 * GRAD_ROWS
    pairs = lax.axis_size("pair")
    chunk = chans // pairs
    half = blocks * count
    params = pltpu.CompilerParams(vmem_limit_bytes=VMEM_LIMIT)
    packed, small = pl.pallas_call(
        pack_kernel,
        out_shape=[
            jax.ShapeDtypeStruct((rows, chans), jnp.bfloat16),
            jax.ShapeDtypeStruct((count + chans, chans), jnp.bfloat16),
        ],
        scratch_shapes=[pltpu.VMEM((GRAD_ROWS, LANES), jnp.float32)],
        name="pack",
    )(one, two, grad, weight)
    with jax.named_scope("frames_across"):
        packed_far = lax.ppermute(packed, "pix", across)
    with jax.named_scope("near_gather"):
        near_keys = lax.all_gather(two, "pix", axis=0, axis_index_groups=near)
    near_feat, near_prob, near_stat, near_turned = pl.pallas_call(
        functools.partial(near_kernel, scale),
        grid=(1,),
        in_specs=[whole(blocks, count, chans), whole(count + chans, chans)],
        out_specs=[whole(half, 2 * chans), whole(count, half), whole(3, count, LANES), whole(2, chans, count)],
        out_shape=[
            jax.ShapeDtypeStruct((half, 2 * chans), jnp.bfloat16),
            jax.ShapeDtypeStruct((count, half), jnp.bfloat16),
            jax.ShapeDtypeStruct((3, count, LANES), jnp.float32),
            jax.ShapeDtypeStruct((2, chans, count), jnp.bfloat16),
        ],
        scratch_shapes=[
            pltpu.VMEM((count, half), jnp.float32),
            pltpu.VMEM((count, chans), jnp.bfloat16),
            pltpu.VMEM((count, LANES), jnp.float32),
        ],
        compiler_params=params,
        cost_estimate=pl.CostEstimate(flops=2 * count * half * chans, bytes_accessed=6 * 2**20, transcendentals=0),
        name="near",
    )(near_keys, small)
    with jax.named_scope("far_gather"):
        far_keys = lax.all_gather(packed_far[0:count], "pix", axis=0, axis_index_groups=near)

    flow, back_one, payload = pl.pallas_call(
        functools.partial(match_kernel, frame_rows, scale),
        grid=(1,),
        in_specs=[
            whole(half, 2 * chans),
            whole(count, half),
            whole(3, count, LANES),
            whole(2, chans, count),
            whole(blocks, count, chans),
            whole(count, chans),
            whole(2, count),
            whole(rows, chans),
            whole(chans, chans),
        ],
        out_specs=[whole(2, count), whole(count, chans), whole(2, blocks // 2, chans, count + chans)],
        out_shape=[
            jax.ShapeDtypeStruct((2, count), jnp.float32),
            jax.ShapeDtypeStruct((count, chans), jnp.bfloat16),
            jax.ShapeDtypeStruct((2, blocks // 2, chans, count + chans), jnp.bfloat16),
        ],
        scratch_shapes=[
            pltpu.VMEM((half, 2 * chans), jnp.bfloat16),
            pltpu.VMEM((count, 2 * half), jnp.float32),
            pltpu.VMEM((count, half), jnp.float32),
            pltpu.VMEM((count, half), jnp.bfloat16),
            pltpu.VMEM((count, half), jnp.bfloat16),
            pltpu.VMEM((count, half), jnp.bfloat16),
            pltpu.VMEM((2 * count, chans), jnp.bfloat16),
            pltpu.VMEM((chans, count), jnp.bfloat16),
            pltpu.VMEM((2 * count, LANES), jnp.float32),
            pltpu.VMEM((2 * count, LANES), jnp.float32),
            pltpu.VMEM((2 * count, LANES), jnp.float32),
            pltpu.VMEM((2 * count, LANES), jnp.float32),
            pltpu.VMEM((3 * count, LANES), jnp.float32),
            pltpu.VMEM((3 * count, LANES), jnp.float32),
            pltpu.VMEM((count, 2 * chans), jnp.float32),
            pltpu.VMEM((count, 2 * chans), jnp.bfloat16),
            pltpu.VMEM((chans, count), jnp.bfloat16),
            pltpu.VMEM((LANES, 2 * count), jnp.float32),
        ],
        compiler_params=params,
        cost_estimate=pl.CostEstimate(flops=6 * 2 * count * 2 * half * chans, bytes_accessed=8 * 2**20, transcendentals=0),
        name="match",
    )(near_feat, near_prob, near_stat, near_turned, far_keys, one, grad, packed_far, weight)

    with jax.named_scope("partial_sums"):
        cores = [[2 * i, 2 * i + 1] for i in range(blocks)]
        chips = [[y * 4 + r for y in range(devices // 4)] for r in range(4)]
        swapped = lax.all_to_all(payload, "pix", 0, 0, axis_index_groups=cores)
        summed = (swapped[0].astype(jnp.float32) + swapped[1].astype(jnp.float32)).astype(jnp.bfloat16)
        arrived = lax.all_to_all(summed, "pix", 0, 0, axis_index_groups=chips)
    with jax.named_scope("weight_terms"):
        term = jnp.sum(arrived[:, :, count:].astype(jnp.float32), axis=0).astype(jnp.bfloat16)
        sent = jnp.repeat(term.reshape(pairs, chunk, chans), 2, axis=0)
        planes = [
            [p * devices + z * 2 + r for p in range(pairs) for z in range(2)]
            for r in [y * 4 + c for y in range(devices // 4) for c in range(2)]
        ]
        terms = lax.all_to_all(sent, ("pair", "pix"), 0, 0, axis_index_groups=planes)
        weight_grad = jnp.sum(terms.astype(jnp.float32), axis=0)

    back_two = pl.pallas_call(
        owner_kernel,
        out_shape=jax.ShapeDtypeStruct((count, chans), jnp.bfloat16),
        cost_estimate=pl.CostEstimate(flops=2 * count * chans * chans, bytes_accessed=2**20, transcendentals=0),
        name="owner",
    )(arrived, weight)
    return (flow[None], back_one[None], back_two[None], weight_grad)


def solution(mesh):
    return jax.shard_map(
        on_device,
        mesh=mesh,
        in_specs=(P("pair", "pix", None), P("pair", "pix", None), P(), P("pair", None, "pix")),
        out_specs=(
            P("pair", None, "pix"),
            P("pair", "pix", None),
            P("pair", "pix", None),
            P("pair", None),
        ),
        check_vma=False,
    )
```

```python
import functools

import jax
import jax.numpy as jnp
from jax import lax
from jax.experimental import pallas as pl
from jax.experimental.pallas import tpu as pltpu
from jax.sharding import PartitionSpec as P

COLS = 128
LANES = 128
SUB = 32
FIRST = 4
SECOND_ROWS = 48
THIRD = 6
GRAD_ROWS = 32
VMEM_LIMIT = 40 * 1024 * 1024
LOG2E = 1.4426950408889634


def dot(a, b, contract):
    return lax.dot_general(a, b, (contract, ((), ())), preferred_element_type=jnp.float32)


def many(low, high, each, step):
    def body(i, _):
        for k in range(each):
            step(low + i * each + k, 0)
        return 0

    lax.fori_loop(0, (high - low) // each, body, 0)


def turned(a):
    return a.astype(jnp.float32).T.astype(jnp.bfloat16)


def lane_iota(rows):
    return lax.broadcasted_iota(jnp.int32, (rows, LANES), 1)


def parted(value):
    high = value.astype(jnp.bfloat16)
    rest = value - high.astype(jnp.float32)
    middle = rest.astype(jnp.bfloat16)
    return high, middle, (rest - middle.astype(jnp.float32)).astype(jnp.bfloat16)


def joined(ref, start):
    block = ref[start : start + GRAD_ROWS, :].astype(jnp.float32)
    return block[0:8, :] + block[8:16, :] + block[16:24, :]


def pack_kernel(one, two, grad, weight, out, small, spread):
    small[0 : one.shape[0], :] = one[...]
    small[one.shape[0] :, :] = weight[...]
    count = one.shape[0]
    wide = count // LANES
    out[0:count, :] = two[...]
    out[count : 2 * count, :] = one[...]
    spread[...] = jnp.zeros_like(spread)
    for which in range(2):
        for j in range(wide):
            spread[which * wide + j : which * wide + j + 1, :] = grad[which : which + 1, j * LANES : (j + 1) * LANES]
    for part, value in enumerate(parted(spread[0:8, :])):
        spread[part * 8 : (part + 1) * 8, :] = value.astype(jnp.float32)
    out[2 * count : 2 * count + GRAD_ROWS, :] = spread[...].astype(jnp.bfloat16)


def frame_row(z, block, row, rows_per_block):
    index = (block // 2) * 4 + block % 2 + 2 * z
    return (index * rows_per_block + row).astype(jnp.float32)


def take_scores(queries, keys, visit, span, top, out_rows, score, score_visit):
    start = pl.multiple_of(visit * span, span)
    chans = queries.shape[1]
    out = dot(queries, keys[pl.ds(start, span), 0:chans], ((1,), (1,)))
    score[:, pl.ds(pl.multiple_of(score_visit * span, span), span)] = out
    best = top[out_rows, :]
    for j in range(span // LANES):
        best = jnp.maximum(best, out[:, j * LANES : (j + 1) * LANES])
    top[out_rows, :] = best


def weigh_rows(score, rows, peak, zs, rows_per_block, unit, kept, keep):
    size = peak.shape[0]
    in_all = jnp.zeros((size, LANES), jnp.float32)
    in_row = jnp.zeros((size, LANES), jnp.float32)
    blocks = len(zs)
    for j in range(blocks * rows_per_block):
        block = j // rows_per_block
        p = jnp.exp2(score[rows, j * LANES : (j + 1) * LANES] * unit - peak)
        in_all = in_all + p
        in_row = in_row + p * frame_row(zs[block][0], zs[block][1], j % rows_per_block, rows_per_block)
        if j < keep:
            kept[rows, j * LANES : (j + 1) * LANES] = p.astype(jnp.bfloat16)
    return in_all, in_row


def near_kernel(scale, near_keys, small, keys, prob, stat, flipped, score, feat, top):
    blocks, count, chans = near_keys.shape
    span, visits = 2 * count, blocks // 2
    rows_per_block = count // COLS
    tiles = blocks * rows_per_block
    unit = scale * LOG2E
    z_hi = (lax.axis_index("pix") // 2) % 2
    w = small[count : count + chans, :]
    feat[...] = dot(small[0:count, :], w, ((1,), (0,))).astype(jnp.bfloat16)
    flipped[0] = turned(feat[...])
    flipped[1] = turned(small[0:count, :])
    top[...] = jnp.full_like(top, -jnp.inf)

    def step(visit, _):
        for half in range(2):
            start = pl.multiple_of(visit * span + half * count, count)
            raw = near_keys[2 * visit + half]
            keys[pl.ds(start, count), 0:chans] = dot(raw, w, ((1,), (0,))).astype(jnp.bfloat16)
            keys[pl.ds(start, count), chans : 2 * chans] = raw
        take_scores(feat[...], keys, visit, span, top, slice(0, count), score, visit)

    many(0, visits, FIRST, step)
    stat[0] = jnp.broadcast_to(jnp.max(top[...], axis=1, keepdims=True) * unit, (count, LANES))
    zs = [(z_hi, block) for block in range(blocks)]

    def weigh(step, _):
        rows = pl.ds(pl.multiple_of(step * SUB, SUB), SUB)
        stat[1, rows, :], stat[2, rows, :] = weigh_rows(score, rows, stat[0, rows, :], zs, rows_per_block, unit, prob, tiles)

    many(0, count // SUB, THIRD, weigh)


def match_kernel(
    frame_rows, scale,
    near_feat, near_prob, near_stat, near_turned, far_keys, q_own, g_own, packed_far, weight,
    flow, back_one, payload,
    keys, score_far, score_own, prob, slope_near, prob_far, feat_q, far_turned, grads, top, total, total_row, base, tilt, both, low, turned_g, wide_grad,
):
    blocks, count, chans = far_keys.shape[0], q_own.shape[0], q_own.shape[1]
    span = 2 * count
    visits = blocks
    rows_per_block = count // COLS
    tiles = 2 * blocks * rows_per_block
    unit = scale * LOG2E
    here = lax.axis_index("pix")
    z_hi = (here // 2) % 2
    w = weight[...]

    feat_q[0:count, :] = dot(q_own[...], w, ((1,), (0,))).astype(jnp.bfloat16)
    feat_q[count : 2 * count, :] = dot(packed_far[count : 2 * count, :], w, ((1,), (0,))).astype(jnp.bfloat16)
    far_turned[...] = turned(feat_q[count : 2 * count, :])
    wide_grad[...] = jnp.zeros_like(wide_grad)
    wide_grad[0:2, 0:count] = g_own[...]
    far_grad = joined(packed_far, 2 * count)
    for which in range(2):
        for j in range(rows_per_block):
            wide_grad[which : which + 1, count + j * LANES : count + (j + 1) * LANES] = far_grad[
                which * rows_per_block + j : which * rows_per_block + j + 1, :
            ]
    grads[...] = wide_grad[...].T

    half_visits = visits // 2
    half = blocks * count
    own, other = slice(0, count), slice(count, 2 * count)
    both_halves = [(z_hi, block) for block in range(blocks)] + [(1 - z_hi, block) for block in range(blocks)]

    def settle(rows):
        top[rows, :] = jnp.broadcast_to(jnp.max(top[rows, :], axis=1, keepdims=True) * unit, (count, LANES))

    top[...] = jnp.full_like(top, -jnp.inf)

    def near_visit(visit, _):
        take_scores(feat_q[other, :], near_feat, visit, span, top, other, score_far, visit)

    def far_visit(visit, _):
        for part in range(2):
            start = pl.multiple_of(visit * span + part * count, count)
            raw = far_keys[2 * visit + part]
            keys[pl.ds(start, count), 0:chans] = dot(raw, w, ((1,), (0,))).astype(jnp.bfloat16)
            keys[pl.ds(start, count), chans : 2 * chans] = raw
        take_scores(feat_q[other, :], keys, visit, span, top, other, score_far, half_visits + visit)

    many(0, half_visits, FIRST, near_visit)
    many(0, half_visits, FIRST, far_visit)
    settle(other)

    def second(visit, _):
        take_scores(feat_q[own, :], keys, visit, span, top, own, score_own, visit)
        size = SECOND_ROWS
        for part in range(count // size // half_visits):
            start = pl.multiple_of((visit * (count // size // half_visits) + part) * size, size)
            rows, q_rows = pl.ds(start, size), pl.ds(count + start, size)
            total[q_rows, :], total_row[q_rows, :] = weigh_rows(
                score_far, rows, top[q_rows, :], both_halves, rows_per_block, unit, prob_far, tiles // 2
            )

    many(0, half_visits, FIRST, second)
    settle(own)

    def third(step, _):
        rows = pl.ds(pl.multiple_of(step * SUB, SUB), SUB)
        total[rows, :], total_row[rows, :] = weigh_rows(
            score_own, rows, top[rows, :], both_halves[blocks:], rows_per_block, unit, prob, tiles // 2
        )

    many(0, count // SUB, THIRD, third)
    peak = jnp.maximum(top[own, :], near_stat[0])
    by_near, by_far = jnp.exp2(near_stat[0] - peak), jnp.exp2(top[own, :] - peak)
    total[own, :] = total[own, :] * by_far + near_stat[1] * by_near
    total_row[own, :] = total_row[own, :] * by_far + near_stat[2] * by_near

    lane = lane_iota(2 * count)
    lane_f = lane.astype(jnp.float32)
    in_all = jnp.sum(total[...], axis=1, keepdims=True)
    mean_x = 2.0 * (jnp.sum(total[...] * lane_f, axis=1, keepdims=True) / in_all) / (COLS - 1) - 1.0
    mean_y = 2.0 * (jnp.sum(total_row[...], axis=1, keepdims=True) / in_all) / (frame_rows - 1) - 1.0
    share = scale / in_all
    grad = grads[...]
    grad_x, grad_y = grad[:, 0:1], grad[:, 1:2]
    center = grad_x * mean_x + grad_y * mean_y
    key_x = 2.0 * lane_f / (COLS - 1) - 1.0
    whole_base = (grad_x * key_x - center) * share
    whole_tilt = jnp.broadcast_to(grad_y * share, (2 * count, LANES))
    base[0:count, :] = whole_base[0:count, :] * by_near
    tilt[0:count, :] = whole_tilt[0:count, :] * by_near
    base[count : 2 * count, :] = whole_base[count : 2 * count, :]
    tilt[count : 2 * count, :] = whole_tilt[count : 2 * count, :]
    base[2 * count : 3 * count, :] = whole_base[0:count, :] * by_far
    tilt[2 * count : 3 * count, :] = whole_tilt[0:count, :] * by_far
    total_row[0:count, :] = jnp.where(lane[0:count, :] == 0, mean_x[0:count, :], mean_y[0:count, :])
    both[...] = jnp.zeros_like(both)

    def slopes(visit, part, source, out):
        z = 1 - z_hi if part == 2 else z_hi
        for j in range(span // LANES):
            at = slice(visit * span + j * LANES, visit * span + (j + 1) * LANES)
            row = frame_row(z, 2 * visit + j // rows_per_block, j % rows_per_block, rows_per_block)
            key_y = 2.0 * row / (frame_rows - 1) - 1.0
            for step in range(count // SUB):
                rows = slice(step * SUB, (step + 1) * SUB)
                q_rows = slice(part * count + step * SUB, part * count + (step + 1) * SUB)
                factor = (base[q_rows, :] + tilt[q_rows, :] * key_y).astype(jnp.bfloat16)
                out[rows, at] = source[rows, at] * factor

    def near_slopes(visit):
        slopes(visit, 0, near_prob, slope_near)
        slopes(visit, 1, prob_far, prob_far)

    def near_collect(visit):
        at = slice(visit * span, (visit + 1) * span)
        both[...] += dot(slope_near[:, at], near_feat[at, :], ((1,), (0,)))
        partial = dot(near_turned[0], slope_near[:, at], ((1,), (0,)))
        partial = partial + dot(far_turned[...], prob_far[:, at], ((1,), (0,)))
        payload[0, visit, :, 0:count] = partial[:, 0:count].astype(jnp.bfloat16)
        payload[1, visit, :, 0:count] = partial[:, count:span].astype(jnp.bfloat16)

    def far_collect(visit):
        at = slice(visit * span, (visit + 1) * span)
        both[...] += dot(prob[:, at], keys[at, :], ((1,), (0,)))

    near_slopes(0)
    for visit in range(half_visits):
        near_collect(visit)
        if visit + 1 < half_visits:
            near_slopes(visit + 1)
        else:
            slopes(0, 2, prob, prob)
    for visit in range(half_visits):
        far_collect(visit)
        if visit + 1 < half_visits:
            slopes(visit + 1, 2, prob, prob)
    low[...] = both[...].astype(jnp.bfloat16)
    turned_g[...] = turned(low[:, chans : 2 * chans])
    back_one[...] = dot(low[:, 0:chans], w, ((1,), (1,))).astype(jnp.bfloat16)
    term = dot(near_turned[1], low[:, 0:chans], ((1,), (0,)))
    term = (term + dot(turned_g[...], feat_q[0:count, :], ((1,), (0,)))).astype(jnp.bfloat16)
    for core in range(2):
        for place in range(blocks // 2):
            payload[core, place, :, count : count + chans] = term

    flipped = total_row[0:count, :].T
    q_lane = lax.broadcasted_iota(jnp.int32, (1, count), 1)
    q_x = 2.0 * (q_lane % COLS).astype(jnp.float32) / (COLS - 1) - 1.0
    q_y = 2.0 * (q_lane // COLS + here * rows_per_block).astype(jnp.float32) / (frame_rows - 1) - 1.0
    flow[0:1, :] = flipped[0:1, :] - q_x
    flow[1:2, :] = flipped[1:2, :] - q_y


def owner_kernel(arrived, weight, back_two):
    count, chans = back_two.shape
    total = arrived[0, :, 0:count].astype(jnp.float32)
    for block in range(1, arrived.shape[0]):
        total = total + arrived[block, :, 0:count].astype(jnp.float32)
    grad_two = total.T.astype(jnp.bfloat16)
    back_two[...] = dot(grad_two, weight[...], ((1,), (1,))).astype(jnp.bfloat16)


def whole(*shape):
    return pl.BlockSpec(shape, lambda i: (0,) * len(shape))


def on_device(frame_one, frame_two, weight, flow_grad):
    _, count, chans = frame_one.shape
    devices = lax.axis_size("pix")
    blocks = devices // 2
    frame_rows = count * devices // COLS
    scale = chans ** (-0.5)
    near = [[i for i in range(devices) if (i // 2) % 2 == z] for z in range(2)]
    across = [(i, i ^ 2) for i in range(devices)]

    one, two, grad = frame_one[0], frame_two[0], flow_grad[0]
    rows = 2 * count + GRAD_ROWS
    pairs = lax.axis_size("pair")
    chunk = chans // pairs
    half = blocks * count
    params = pltpu.CompilerParams(vmem_limit_bytes=VMEM_LIMIT)
    packed, small = pl.pallas_call(
        pack_kernel,
        out_shape=[
            jax.ShapeDtypeStruct((rows, chans), jnp.bfloat16),
            jax.ShapeDtypeStruct((count + chans, chans), jnp.bfloat16),
        ],
        scratch_shapes=[pltpu.VMEM((GRAD_ROWS, LANES), jnp.float32)],
        name="pack",
    )(one, two, grad, weight)
    with jax.named_scope("frames_across"):
        packed_far = lax.ppermute(packed, "pix", across)
    with jax.named_scope("near_gather"):
        near_keys = lax.all_gather(two, "pix", axis=0, axis_index_groups=near)
    near_feat, near_prob, near_stat, near_turned = pl.pallas_call(
        functools.partial(near_kernel, scale),
        grid=(1,),
        in_specs=[whole(blocks, count, chans), whole(count + chans, chans)],
        out_specs=[whole(half, 2 * chans), whole(count, half), whole(3, count, LANES), whole(2, chans, count)],
        out_shape=[
            jax.ShapeDtypeStruct((half, 2 * chans), jnp.bfloat16),
            jax.ShapeDtypeStruct((count, half), jnp.bfloat16),
            jax.ShapeDtypeStruct((3, count, LANES), jnp.float32),
            jax.ShapeDtypeStruct((2, chans, count), jnp.bfloat16),
        ],
        scratch_shapes=[
            pltpu.VMEM((count, half), jnp.float32),
            pltpu.VMEM((count, chans), jnp.bfloat16),
            pltpu.VMEM((count, LANES), jnp.float32),
        ],
        compiler_params=params,
        cost_estimate=pl.CostEstimate(flops=2 * count * half * chans, bytes_accessed=6 * 2**20, transcendentals=0),
        name="near",
    )(near_keys, small)
    with jax.named_scope("far_gather"):
        far_keys = lax.all_gather(packed_far[0:count], "pix", axis=0, axis_index_groups=near)

    flow, back_one, payload = pl.pallas_call(
        functools.partial(match_kernel, frame_rows, scale),
        grid=(1,),
        in_specs=[
            whole(half, 2 * chans),
            whole(count, half),
            whole(3, count, LANES),
            whole(2, chans, count),
            whole(blocks, count, chans),
            whole(count, chans),
            whole(2, count),
            whole(rows, chans),
            whole(chans, chans),
        ],
        out_specs=[whole(2, count), whole(count, chans), whole(2, blocks // 2, chans, count + chans)],
        out_shape=[
            jax.ShapeDtypeStruct((2, count), jnp.float32),
            jax.ShapeDtypeStruct((count, chans), jnp.bfloat16),
            jax.ShapeDtypeStruct((2, blocks // 2, chans, count + chans), jnp.bfloat16),
        ],
        scratch_shapes=[
            pltpu.VMEM((half, 2 * chans), jnp.bfloat16),
            pltpu.VMEM((count, 2 * half), jnp.float32),
            pltpu.VMEM((count, half), jnp.float32),
            pltpu.VMEM((count, half), jnp.bfloat16),
            pltpu.VMEM((count, half), jnp.bfloat16),
            pltpu.VMEM((count, half), jnp.bfloat16),
            pltpu.VMEM((2 * count, chans), jnp.bfloat16),
            pltpu.VMEM((chans, count), jnp.bfloat16),
            pltpu.VMEM((2 * count, LANES), jnp.float32),
            pltpu.VMEM((2 * count, LANES), jnp.float32),
            pltpu.VMEM((2 * count, LANES), jnp.float32),
            pltpu.VMEM((2 * count, LANES), jnp.float32),
            pltpu.VMEM((3 * count, LANES), jnp.float32),
            pltpu.VMEM((3 * count, LANES), jnp.float32),
            pltpu.VMEM((count, 2 * chans), jnp.float32),
            pltpu.VMEM((count, 2 * chans), jnp.bfloat16),
            pltpu.VMEM((chans, count), jnp.bfloat16),
            pltpu.VMEM((LANES, 2 * count), jnp.float32),
        ],
        compiler_params=params,
        cost_estimate=pl.CostEstimate(flops=6 * 2 * count * 2 * half * chans, bytes_accessed=8 * 2**20, transcendentals=0),
        name="match",
    )(near_feat, near_prob, near_stat, near_turned, far_keys, one, grad, packed_far, weight)

    with jax.named_scope("partial_sums"):
        cores = [[2 * i, 2 * i + 1] for i in range(blocks)]
        chips = [[y * 4 + r for y in range(devices // 4)] for r in range(4)]
        swapped = lax.all_to_all(payload, "pix", 0, 0, axis_index_groups=cores)
        summed = (swapped[0].astype(jnp.float32) + swapped[1].astype(jnp.float32)).astype(jnp.bfloat16)
        arrived = lax.all_to_all(summed, "pix", 0, 0, axis_index_groups=chips)
    with jax.named_scope("weight_terms"):
        term = jnp.sum(arrived[:, :, count:].astype(jnp.float32), axis=0).astype(jnp.bfloat16)
        sent = jnp.repeat(term.reshape(pairs, chunk, chans), 2, axis=0)
        planes = [
            [p * devices + z * 2 + r for p in range(pairs) for z in range(2)]
            for r in [y * 4 + c for y in range(devices // 4) for c in range(2)]
        ]
        terms = lax.all_to_all(sent, ("pair", "pix"), 0, 0, axis_index_groups=planes)
        weight_grad = jnp.sum(terms.astype(jnp.float32), axis=0)

    back_two = pl.pallas_call(
        owner_kernel,
        out_shape=jax.ShapeDtypeStruct((count, chans), jnp.bfloat16),
        cost_estimate=pl.CostEstimate(flops=2 * count * chans * chans, bytes_accessed=2**20, transcendentals=0),
        name="owner",
    )(arrived, weight)
    return (flow[None], back_one[None], back_two[None], weight_grad)


def solution(mesh):
    return jax.shard_map(
        on_device,
        mesh=mesh,
        in_specs=(P("pair", "pix", None), P("pair", "pix", None), P(), P("pair", None, "pix")),
        out_specs=(
            P("pair", None, "pix"),
            P("pair", "pix", None),
            P("pair", "pix", None),
            P("pair", None),
        ),
        check_vma=False,
    )
```
